32 devices in a mesh: dp: 8 (over y, x, core), etp: 4 (over z).
Axes of the slice: x: 2, y: 2, z: 4, core: 2. Of those that a mesh axis runs over, the one named last changes fastest.
Arguments:
- tokens: bfloat16 [4096, 3072], P(('dp', 'etp')), may hold values from -6 to 6
- out_grad: bfloat16 [4096, 3072], P(('dp', 'etp')), may hold values from -4 to 4
- route_ids: int32 [4096, 2], P(('dp', 'etp')), may hold values from 0 to 7, as said below
- route_prob: bfloat16 [4096], P(('dp', 'etp')), may hold values from 0.19921875 to 1
- w_gate: bfloat16 [3072, 8192], P(None, 'etp'), may hold values from -0.109375 to 0.109375
- w_up: bfloat16 [3072, 8192], P(None, 'etp'), may hold values from -0.109375 to 0.109375
- w_down: bfloat16 [8192, 3072], P('etp'), may hold values from -0.0625 to 0.0625
Outputs:
- grad_tokens: bfloat16 [4096, 3072], P(('dp', 'etp'))
- grad_prob: float32 [4096], P(('dp', 'etp'))
- grad_gate: bfloat16 [3072, 8192], P('dp', 'etp')
- grad_up: bfloat16 [3072, 8192], P('dp', 'etp')
- grad_down: bfloat16 [8192, 3072], P('etp', 'dp')
The draws below stay inside these ranges and needn't reach their ends.
Inputs may be any that keep to these rules, and one draw needn't show every extreme that they name: `route_ids`: each row names two different experts. In each aligned block of 128 rows (the rows of one device) between 24 and 32 rows name expert 0, and in some block exactly 32 rows do.
All inputs are finite; a program needn't handle non-finite values.
Results may differ from the reference program's by a relative error of at most 0.023.
Values may be sent and summed in bfloat16 or wider, within the bound.
No kernel may reach another device: no remote copies, remote signals or barrier semaphores. Data moves between devices by JAX's collectives and lax.ppermute only.
A program may use at most 256 MiB of HBM per device.

```python
import jax
import jax.numpy as jnp
from jax import lax

D = 3072
FF = 8192
EXPERTS = 8
TOK_DEV = 128
LOC_CAP = 32
TOKENS = 4096
N_DP = 8
N_ETP = 4


def draw_route_ids(key, part):
    key = jax.random.fold_in(key, 11)
    subkeys = jax.random.split(key, 6)
    blocks = TOKENS // TOK_DEV
    counts = jax.random.randint(subkeys[0], (blocks,), LOC_CAP * 3 // 4, LOC_CAP + 1)
    fullest = jax.random.randint(subkeys[1], (), 0, blocks)
    counts = jnp.where(jnp.arange(blocks) == fullest, LOC_CAP, counts)
    ranking = jax.vmap(lambda sub_key: jax.random.permutation(sub_key, TOK_DEV))(jax.random.split(subkeys[2], blocks))
    chosen = ranking < counts[:, None]
    primary = jax.random.randint(subkeys[3], (blocks, TOK_DEV), 1, EXPERTS)
    step_off = jax.random.randint(subkeys[4], (blocks, TOK_DEV), 1, EXPERTS - 1)
    secondary = 1 + (primary - 1 + step_off) % (EXPERTS - 1)
    placing = jax.random.randint(subkeys[5], (blocks, TOK_DEV), 0, 2)
    slot_a = jnp.where(chosen, jnp.where(placing == 0, 0, primary), primary)
    slot_b = jnp.where(chosen, jnp.where(placing == 0, primary, 0), secondary)
    return jnp.stack([slot_a, slot_b], axis=-1).reshape(TOKENS, 2).astype(jnp.int32)


def spiked(array, stream_key, source, target, blocks, factor):
    owner, partner = [(jnp.arange(array.shape[position]) // (array.shape[position] // blocks)).reshape([-1 if axis == position else 1 for axis in range(array.ndim)]) for position in (source, target)]
    chosen = jax.random.permutation(stream_key, blocks)[partner]
    strong = (owner == chosen) | (owner == (partner + blocks // 2) % blocks)
    return jnp.where(strong, factor * array, array)


def level_of(own_key, extent, pieces, least, high):
    level, own = 1.0, jax.random.fold_in(own_key, 6)
    for axis_at, blocks in pieces:
        heights = jnp.exp(jax.random.uniform(jax.random.fold_in(own, axis_at), (blocks,), jnp.float32, least / len(pieces), high / len(pieces)))
        level = level * jnp.repeat(heights, extent[axis_at] // blocks).reshape([-1 if axis == axis_at else 1 for axis in range(len(extent))])
    return level


def normal_values(key, extent, width, reach, pieces=(), kind=jnp.bfloat16):
    array = width * jax.random.normal(key, extent, jnp.float32)
    if pieces:
        array = array * level_of(key, extent, pieces, -0.22, 0.18)
    return jnp.clip(array, -reach, reach).astype(kind)


def heavy_noise(key, dims, deviation, limit, shards, heavy, kind=jnp.bfloat16):
    array = deviation * jax.random.normal(key, dims, jnp.float32)
    if shards:
        array = array * level_of(key, dims, shards, -0.22, 0.18)
    return jnp.clip(spiked(array, jax.random.fold_in(key, 3), *heavy), -limit, limit).astype(kind)


def setup_inputs(seed: int = 0) -> dict:
    key_of = jax.random.split(jax.random.key(seed), 8)
    tokens = heavy_noise(key_of[0], (TOKENS, D), 1.0, 6.0, ((0, 32),), (0, 1, 32, 2.75))
    out_grad = normal_values(key_of[1], (TOKENS, D), 0.5, 4.0, ((0, 32),))
    route_ids = draw_route_ids(jax.random.fold_in(key_of[7], 71), 0)
    route_prob = jnp.clip(0.19921875 + 0.80078125 * jax.random.uniform(key_of[3], (TOKENS,), jnp.float32) ** level_of(key_of[3], (TOKENS,), ((0, 32),), -0.2, 0.2), 0.19921875, 1.0).astype(jnp.bfloat16)
    w_gate = normal_values(key_of[4], (D, FF), D ** -0.5, 0.109375, ((1, 4),))
    w_up = normal_values(key_of[5], (D, FF), D ** -0.5, 0.109375, ((1, 4),))
    w_down = normal_values(key_of[6], (FF, D), FF ** -0.5, 0.0625, ((0, 4),))
    return {"tokens": tokens, "out_grad": out_grad, "route_ids": route_ids, "route_prob": route_prob, "w_gate": w_gate, "w_up": w_up, "w_down": w_down}


def reference(tokens, out_grad, route_ids, route_prob, w_gate, w_up, w_down):
    total = tokens.shape[0]
    model_width = tokens.shape[1]
    block_width = FF // N_ETP
    slots = N_DP * N_ETP * LOC_CAP
    routed = jnp.logical_or(route_ids[:, 0] == 0, route_ids[:, 1] == 0)
    positions = jnp.arange(total, dtype=jnp.int32)
    packed_order = jnp.argsort(jnp.where(routed, positions, positions + total))[:slots].astype(jnp.int32)
    x_rows = tokens[packed_order]
    dy_rows = out_grad[packed_order]
    row_weight = jnp.where(routed, route_prob, jnp.zeros_like(route_prob))[packed_order]
    row_scale = row_weight.astype(jnp.float32)[:, None]
    gate_blocks = w_gate.reshape(model_width, N_ETP, block_width).transpose(1, 0, 2)
    up_blocks = w_up.reshape(model_width, N_ETP, block_width).transpose(1, 0, 2)
    down_blocks = w_down.reshape(N_ETP, block_width, model_width)

    def one_block(carry, blocks):
        token_acc, prob_acc = carry
        gate_w, up_w, down_w = blocks
        gate_pre = jnp.dot(x_rows, gate_w, preferred_element_type=jnp.float32)
        up_pre = jnp.dot(x_rows, up_w, preferred_element_type=jnp.float32)
        sig_gate = jax.nn.sigmoid(gate_pre)
        act_gate = gate_pre * sig_gate
        hidden = (act_gate * up_pre).astype(jnp.bfloat16)
        scaled = (row_scale * hidden.astype(jnp.float32)).astype(jnp.bfloat16)
        hidden_raw = jnp.dot(dy_rows, down_w.T, preferred_element_type=jnp.float32)
        prob_acc = prob_acc + jnp.sum(hidden.astype(jnp.float32) * hidden_raw, axis=1)
        grad_hidden = row_scale * hidden_raw
        grad_gate_pre = (grad_hidden * up_pre * sig_gate * (1.0 + gate_pre * (1.0 - sig_gate))).astype(jnp.bfloat16)
        grad_up_pre = (grad_hidden * act_gate).astype(jnp.bfloat16)
        token_part = jnp.dot(grad_gate_pre, gate_w.T, preferred_element_type=jnp.float32)
        token_part = token_part + jnp.dot(grad_up_pre, up_w.T, preferred_element_type=jnp.float32)
        token_part = lax.optimization_barrier(token_part.astype(jnp.bfloat16)).astype(jnp.float32)
        gate_grad = jnp.dot(x_rows.T, grad_gate_pre, preferred_element_type=jnp.float32)
        up_grad = jnp.dot(x_rows.T, grad_up_pre, preferred_element_type=jnp.float32)
        down_grad = jnp.dot(scaled.T, dy_rows, preferred_element_type=jnp.float32)
        return (token_acc + token_part, prob_acc), (gate_grad, up_grad, down_grad)

    start_carry = (jnp.zeros((slots, model_width), jnp.float32), jnp.zeros((slots,), jnp.float32))
    (token_acc, prob_acc), (gate_parts, up_parts, down_parts) = lax.scan(
        one_block, start_carry, (gate_blocks, up_blocks, down_blocks))
    grad_gate = (gate_parts.transpose(1, 0, 2).reshape(model_width, FF) / N_DP).astype(jnp.bfloat16)
    grad_up = (up_parts.transpose(1, 0, 2).reshape(model_width, FF) / N_DP).astype(jnp.bfloat16)
    grad_down = (down_parts.reshape(FF, model_width) / N_DP).astype(jnp.bfloat16)
    grad_tokens = jnp.zeros((total, model_width), jnp.bfloat16).at[packed_order].set(token_acc.astype(jnp.bfloat16))
    live_rows = routed[packed_order].astype(jnp.float32)
    grad_prob = jnp.zeros((total,), jnp.float32).at[packed_order].set(prob_acc * live_rows)
    return grad_tokens, grad_prob, grad_gate, grad_up, grad_down
```

```python
import jax
import jax.numpy as jnp
from jax import lax
from jax.sharding import PartitionSpec as P

LOC_CAP = 32
LANES = 128


def contract_rows(left, right):
    return lax.dot_general(
        left, right, (((0,), (0,)), ((), ())), preferred_element_type=jnp.float32
    )


def contract_cols(left, right):
    return lax.dot_general(
        left, right, (((1,), (1,)), ((), ())), preferred_element_type=jnp.float32
    )


def shift(block, step):
    ways = lax.axis_size("etp")
    return lax.ppermute(block, "etp", [(i, (i + step) % ways) for i in range(ways)])


def exchange(block, bit):
    ways = lax.axis_size("dp")
    return lax.ppermute(block, "dp", [(i, i ^ bit) for i in range(ways)])


def ring_blocks(block):
    ways = lax.axis_size("etp")
    return [block] + [shift(block, step) for step in range(1, ways)]


def dp_gather(block):
    ways = lax.axis_size("dp")
    bits = [1 << k for k in range(ways.bit_length() - 1)]
    half = block.shape[1] // 2
    halves = []
    for part, order in (
        (block[:, :half], bits[1:] + bits[:1]),
        (block[:, half:], bits[:0:-1] + bits[:1]),
    ):
        held = {0: part}
        for bit in order:
            keys = sorted(held)
            sent = jnp.concatenate([held[key] for key in keys], axis=0)
            got = exchange(sent, bit)
            rows = part.shape[0]
            for at, key in enumerate(keys):
                held[key ^ bit] = got[at * rows : (at + 1) * rows]
        halves.append(jnp.concatenate([held[key] for key in range(ways)], axis=0))
    return halves


def dp_slices(rows):
    ways = lax.axis_size("dp")
    me = lax.axis_index("dp")
    every = lax.all_to_all(rows, "dp", split_axis=1, concat_axis=0, tiled=True)
    every = every.reshape(ways, rows.shape[0], -1)
    return jnp.concatenate(
        [lax.dynamic_index_in_dim(every, me ^ k, 0, keepdims=False) for k in range(ways)], axis=0
    )


def shards(tokens, out_grad, route_ids, route_prob, w_gate, w_up, w_down):
    tok_rows = tokens.shape[0]
    width = tokens.shape[1]
    data_ways = lax.axis_size("dp")
    etp_ways = lax.axis_size("etp")
    routed = jnp.logical_or(route_ids[:, 0] == 0, route_ids[:, 1] == 0)
    positions = jnp.arange(tok_rows, dtype=jnp.int32)
    before = (positions[:, None] <= positions[None, :]) & routed[:, None]
    slot = jnp.sum(before.astype(jnp.int32), axis=0) - 1
    matches = (slot[None, :] == jnp.arange(LOC_CAP, dtype=jnp.int32)[:, None]) & routed[None, :]
    selector = matches.astype(jnp.bfloat16)
    x_pack = jnp.dot(selector, tokens, preferred_element_type=jnp.float32).astype(jnp.bfloat16)
    dy_pack = jnp.dot(selector, out_grad, preferred_element_type=jnp.float32).astype(jnp.bfloat16)
    w_pack = jnp.sum(
        jnp.where(matches, route_prob.astype(jnp.float32)[None, :], 0.0), axis=1
    ).astype(jnp.bfloat16)
    x_ext = jnp.concatenate(
        [x_pack, jnp.broadcast_to(w_pack[:, None], (LOC_CAP, LANES))], axis=1
    )
    x_ext = jnp.concatenate(ring_blocks(x_ext), axis=0)
    dy_all = jnp.concatenate(ring_blocks(dy_pack), axis=0)
    x_all = x_ext[:, :width]
    row_scale = x_ext[:, width : width + 1].astype(jnp.float32)

    gate_pre = jnp.dot(x_all, w_gate, preferred_element_type=jnp.float32)
    up_pre = jnp.dot(x_all, w_up, preferred_element_type=jnp.float32)
    sig_gate = jax.nn.sigmoid(gate_pre)
    act_gate = gate_pre * sig_gate
    hidden = (act_gate * up_pre).astype(jnp.bfloat16)
    scaled = (row_scale * hidden.astype(jnp.float32)).astype(jnp.bfloat16)
    scaled_all = dp_gather(scaled)
    x_slice = dp_slices(x_all)

    hidden_raw = contract_cols(dy_all, w_down)
    grad_hidden = row_scale * hidden_raw
    grad_gate_pre = (grad_hidden * up_pre * sig_gate * (1.0 + gate_pre * (1.0 - sig_gate))).astype(
        jnp.bfloat16
    )
    grad_up_pre = (grad_hidden * act_gate).astype(jnp.bfloat16)
    gate_all = dp_gather(grad_gate_pre)
    up_all = dp_gather(grad_up_pre)
    dy_slice = dp_slices(dy_all)

    prob_part = jnp.sum(hidden.astype(jnp.float32) * hidden_raw, axis=1, keepdims=True)
    prob_hi = prob_part.astype(jnp.bfloat16)
    prob_rest = prob_part - prob_hi.astype(jnp.float32)
    prob_mid = prob_rest.astype(jnp.bfloat16)
    prob_lo = (prob_rest - prob_mid.astype(jnp.float32)).astype(jnp.bfloat16)
    token_part = (
        contract_cols(grad_gate_pre, w_gate) + contract_cols(grad_up_pre, w_up)
    ).astype(jnp.bfloat16)
    token_ext = jnp.concatenate(
        [token_part, prob_hi, prob_mid, prob_lo, jnp.zeros((token_part.shape[0], LANES - 3), jnp.bfloat16)],
        axis=1,
    )
    share = token_ext[:LOC_CAP].astype(jnp.float32)
    for step in range(1, etp_ways):
        share = share + shift(token_ext[step * LOC_CAP : (step + 1) * LOC_CAP], -step).astype(jnp.float32)
    token_share = share[:, :width].astype(jnp.bfloat16)
    prob_share = share[:, width] + share[:, width + 1] + share[:, width + 2]
    spread_prob = jnp.where(matches, prob_share[:, None], jnp.zeros_like(prob_share)[:, None])
    grad_prob = jnp.sum(spread_prob, axis=0)
    grad_tokens = contract_rows(selector, token_share).astype(jnp.bfloat16)

    inv = 1.0 / data_ways
    grad_down = jnp.concatenate(
        [(contract_rows(part, dy_slice) * inv).astype(jnp.bfloat16) for part in scaled_all], axis=0
    )
    grad_gate, grad_up = (
        jnp.concatenate(
            [(contract_rows(x_slice, part) * inv).astype(jnp.bfloat16) for part in parts], axis=1
        )
        for parts in (gate_all, up_all)
    )
    return (grad_tokens, grad_prob, grad_gate, grad_up, grad_down)


def solution(mesh):
    placed = (
        P(("dp", "etp"), None),
        P(("dp", "etp"), None),
        P(("dp", "etp"), None),
        P(("dp", "etp")),
        P(None, "etp"),
        P(None, "etp"),
        P("etp", None),
    )
    return jax.shard_map(
        shards,
        mesh=mesh,
        in_specs=placed,
        out_specs=(
            P(("dp", "etp"), None),
            P(("dp", "etp")),
            P("dp", "etp"),
            P("dp", "etp"),
            P("etp", "dp"),
        ),
        check_vma=False,
    )
```

```python
import functools

import jax
import jax.numpy as jnp
from jax import lax
from jax.experimental import pallas as pl
from jax.experimental.pallas import tpu as pltpu
from jax.sharding import PartitionSpec as P

LOC_CAP = 32
LANES = 128
BLOCK = 256
MIB = 1024 * 1024
BF16 = jnp.bfloat16
F32 = jnp.float32
IN_VMEM = pl.BlockSpec(memory_space=pltpu.VMEM)
IN_HBM = pl.BlockSpec(memory_space=pltpu.HBM)
IN_SMEM = pl.BlockSpec(memory_space=pltpu.SMEM)


def call(body, name, out_shape, in_specs, flops, moved, scratch=(), limit=12, **kwargs):
    if "out_specs" not in kwargs:
        kwargs["out_specs"] = jax.tree.map(lambda _: IN_VMEM, out_shape)
    return pl.pallas_call(
        body,
        out_shape=out_shape,
        in_specs=in_specs,
        scratch_shapes=scratch,
        compiler_params=pltpu.CompilerParams(vmem_limit_bytes=limit * MIB),
        cost_estimate=pl.CostEstimate(
            flops=int(flops), bytes_accessed=int(moved), transcendentals=0
        ),
        name=name,
        **kwargs,
    )


def struct(shape, kind=BF16):
    return jax.ShapeDtypeStruct(shape, kind)


def nt_dot(left, right):
    return lax.dot_general(left, right, (((1,), (1,)), ((), ())), preferred_element_type=F32)


def shift(block, step):
    ways = lax.axis_size("etp")
    return lax.ppermute(block, "etp", [(i, (i + step) % ways) for i in range(ways)])


def exchange(block, bits):
    ways = lax.axis_size("dp")
    return lax.ppermute(block, "dp", [(i, i ^ bits) for i in range(ways)])


def chip_gather(piece, chips):
    rows = piece.shape[0] // 2
    held = {0: [piece]}
    for key in sorted(range(1, chips), key=lambda k: (k.bit_count(), k)):
        if key.bit_count() == 1:
            held[key] = [exchange(piece, 2 * key)]
            continue
        high, low = 1 << (key.bit_length() - 1), key & -key
        upper, lower = held[key ^ high], held[key ^ low]
        upper = upper[0] if len(upper) == 2 else upper[0][:rows]
        lower = lower[1] if len(lower) == 2 else lower[0][rows:]
        held[key] = [exchange(upper, 2 * high), exchange(lower, 2 * low)]
    return [held[key] for key in range(chips)]


def pack_x_body(ids_ref, prob_ref, tokens_ref, x_ref, sel_ref):
    rows, width = tokens_ref.shape
    ids = ids_ref[...]
    routed = jnp.logical_or(ids[0:1] == 0, ids[1:2] == 0)
    flags = jnp.broadcast_to(routed.astype(F32), (8, rows)).astype(BF16)
    upto = (
        lax.broadcasted_iota(jnp.int32, (rows, rows), 0)
        <= lax.broadcasted_iota(jnp.int32, (rows, rows), 1)
    ).astype(F32).astype(BF16)
    slot = jnp.dot(flags, upto, preferred_element_type=F32)[0:1].astype(jnp.int32) - 1
    slots = lax.broadcasted_iota(jnp.int32, (LOC_CAP, rows), 0)
    matches = jnp.logical_and(slots == slot, routed)
    sel = matches.astype(F32)
    weight = jnp.sum(sel * prob_ref[...].astype(F32), axis=1, keepdims=True)
    sel = sel.astype(BF16)
    sel_ref[...] = sel
    x_ref[:, :width] = jnp.dot(sel, tokens_ref[...], preferred_element_type=F32).astype(BF16)
    x_ref[:, width:] = jnp.broadcast_to(weight, (LOC_CAP, LANES)).astype(BF16)


def pack_x(ids, prob, tokens):
    rows, width = tokens.shape
    return call(
        pack_x_body,
        "pack_x",
        [struct((LOC_CAP, width + LANES)), struct((LOC_CAP, rows))],
        [IN_VMEM] * 3,
        2 * LOC_CAP * rows * width,
        2 * rows * width,
    )(ids, prob, tokens)


def pack_dy_body(chips, chip_ref, sel_ref, grad_ref, dy_ref, *slice_refs):
    dy_ref[...] = jnp.dot(sel_ref[...], grad_ref[...], preferred_element_type=F32).astype(BF16)
    part = slice_refs[0].shape[1]
    for key in range(chips):
        first = pl.multiple_of((chip_ref[0] ^ key) * part, LANES)
        slice_refs[key][...] = dy_ref[:, pl.ds(first, part)]


def pack_dy(chip, sel, out_grad, chips):
    rows, width = out_grad.shape
    return call(
        functools.partial(pack_dy_body, chips),
        "pack_dy",
        [struct((LOC_CAP, width))] + [struct((LOC_CAP, width // chips))] * chips,
        [IN_SMEM] + [IN_VMEM] * 2,
        2 * LOC_CAP * rows * width,
        2 * rows * width,
    )(chip, sel, out_grad)


def join_x_body(chips, count, chip_ref, *refs):
    blocks, x_ref, slice_refs = refs[:count], refs[count], refs[count + 1 :]
    part = slice_refs[0].shape[1]
    for at, block in enumerate(blocks):
        x_ref[at * LOC_CAP : (at + 1) * LOC_CAP, :] = block[...]
    for key in range(chips):
        first = pl.multiple_of((chip_ref[0] ^ key) * part, LANES)
        slice_refs[key][...] = x_ref[:, pl.ds(first, part)]


def join_x(chip, blocks, chips):
    count = len(blocks)
    wide = blocks[0].shape[1]
    rows = count * LOC_CAP
    part = (wide - LANES) // chips
    return call(
        functools.partial(join_x_body, chips, count),
        "join_x",
        [struct((rows, wide))] + [struct((rows, part))] * chips,
        [IN_SMEM] + [IN_VMEM] * count,
        0,
        4 * rows * wide,
    )(chip, *blocks)


def windowed(groups, sems, ahead):
    made, at = [], 0
    for group in groups:
        made.append(
            [pltpu.make_async_copy(src, dst, sems.at[at + k]) for k, (src, dst) in enumerate(group)]
        )
        at += len(group)
    for copies in made[:ahead]:
        for copy in copies:
            copy.start()
    for step, copies in enumerate(made):
        for copy in copies:
            copy.wait()
        if step + ahead < len(made):
            for copy in made[step + ahead]:
                copy.start()
        yield step


def forward_body(
    x_ref, gate_hbm, up_hbm, scaled_ref, hidden_ref, silu_ref, slope_ref, gate_ref, up_ref, sems
):
    width, units = gate_hbm.shape
    x = x_ref[:, :width]
    weight = x_ref[:, width : width + 1].astype(F32)
    spans = [pl.ds(at, BLOCK) for at in range(0, units, BLOCK)]
    groups = [
        [(gate_hbm.at[:, span], gate_ref.at[:, span]), (up_hbm.at[:, span], up_ref.at[:, span])]
        for span in spans
    ]
    for step in windowed(groups, sems, 3):
        cols = slice(step * BLOCK, (step + 1) * BLOCK)
        gate = jnp.dot(x, gate_ref[:, cols], preferred_element_type=F32)
        up = jnp.dot(x, up_ref[:, cols], preferred_element_type=F32)
        sig = 1.0 / (1.0 + jnp.exp(-gate))
        act = gate * sig
        hidden = (act * up).astype(BF16)
        hidden_ref[:, cols] = hidden
        scaled_ref[:, cols] = (weight * hidden.astype(F32)).astype(BF16)
        silu_ref[:, cols] = weight * act
        slope_ref[:, cols] = weight * up * sig * (1.0 + gate * (1.0 - sig))


def forward(x_all, w_gate, w_up):
    rows = x_all.shape[0]
    width, units = w_gate.shape
    return call(
        forward_body,
        "forward",
        [struct((rows, units), kind) for kind in (BF16, BF16, F32, F32)],
        [IN_VMEM] + [IN_HBM] * 2,
        4 * rows * width * units,
        4 * width * units,
        [pltpu.VMEM(w_gate.shape, BF16)] * 2 + [pltpu.SemaphoreType.DMA((2 * (units // BLOCK),))],
        limit=54,
    )(x_all, w_gate, w_up)


def backward_body(count, *refs):
    blocks = refs[:count]
    down_hbm, hidden_ref, silu_ref, slope_ref, grad_ref, prob_ref, down_ref, sems = refs[count:]
    rows, units = hidden_ref.shape
    spans = [pl.ds(at, BLOCK) for at in range(0, units, BLOCK)]
    groups = [[(down_hbm.at[span], down_ref.at[span])] for span in spans]
    dy = jnp.concatenate([block[...] for block in blocks], axis=0)
    prob = jnp.zeros((rows, 1), F32)
    for step in windowed(groups, sems, 5):
        at = step * BLOCK
        cols = slice(at, at + BLOCK)
        raw = nt_dot(dy, down_ref[cols, :])
        grad_ref[:, cols] = (raw * slope_ref[:, cols]).astype(BF16)
        grad_ref[:, units + at : units + at + BLOCK] = (raw * silu_ref[:, cols]).astype(BF16)
        prob = prob + jnp.sum(hidden_ref[:, cols].astype(F32) * raw, axis=1, keepdims=True)
    prob_ref[...] = prob


def backward(dy_blocks, w_down, hidden, silu, slope):
    count = len(dy_blocks)
    rows, units = hidden.shape
    width = w_down.shape[1]
    return call(
        functools.partial(backward_body, count),
        "backward",
        [struct((rows, 2 * units)), struct((rows, 1), F32)],
        [IN_VMEM] * count + [IN_HBM] + [IN_VMEM] * 3,
        2 * rows * width * units,
        2 * width * units + 12 * rows * units,
        [pltpu.VMEM(w_down.shape, BF16), pltpu.SemaphoreType.DMA((units // BLOCK,))],
        limit=54,
    )(*dy_blocks, w_down, hidden, silu, slope)


def token_body(count, gate_hbm, up_hbm, grad_ref, prob_ref, *refs):
    outs = refs[:count]
    gate_w, up_w, sems = refs[count:]
    width, units = gate_hbm.shape
    spans = [pl.ds(at, BLOCK) for at in range(0, width, BLOCK)]
    groups = [
        [(gate_hbm.at[span], gate_w.at[span]), (up_hbm.at[span], up_w.at[span])] for span in spans
    ]
    prob = prob_ref[...]
    high = prob.astype(BF16).astype(F32)
    mid = (prob - high).astype(BF16).astype(F32)
    low = prob - high - mid
    lane = lax.broadcasted_iota(jnp.int32, (prob.shape[0], LANES), 1)
    terms = jnp.where(
        lane == 0, high, jnp.where(lane == 1, mid, jnp.where(lane == 2, low, 0.0))
    ).astype(BF16)
    for z in range(count):
        outs[z][:, width:] = terms[z * LOC_CAP : (z + 1) * LOC_CAP]
    gate = grad_ref[:, :units]
    up = grad_ref[:, units:]
    for step in windowed(groups, sems, 4):
        cols = slice(step * BLOCK, (step + 1) * BLOCK)
        share = (nt_dot(gate, gate_w[cols, :]) + nt_dot(up, up_w[cols, :])).astype(BF16)
        for z in range(count):
            outs[z][:, cols] = share[z * LOC_CAP : (z + 1) * LOC_CAP]


def token_shares(w_gate, w_up, grad, prob, count):
    width, units = w_gate.shape
    rows = count * LOC_CAP
    return call(
        functools.partial(token_body, count),
        "token_shares",
        [struct((LOC_CAP, width + LANES))] * count,
        [IN_HBM] * 2 + [IN_VMEM] * 2,
        4 * rows * width * units,
        4 * width * units,
        [pltpu.VMEM(w_gate.shape, BF16)] * 2 + [pltpu.SemaphoreType.DMA((2 * (width // BLOCK),))],
        limit=54,
    )(w_gate, w_up, grad, prob)


def place_body(*refs):
    shares, sel_ref, tokens_ref, prob_ref = refs[:-3], refs[-3], refs[-2], refs[-1]
    width = tokens_ref.shape[1]
    total = shares[0][...].astype(F32)
    for share in shares[1:]:
        total = total + share[...].astype(F32)
    rows = total[:, :width].astype(BF16)
    sel = sel_ref[...]
    tokens_ref[...] = lax.dot_general(
        sel, rows, (((0,), (0,)), ((), ())), preferred_element_type=F32
    ).astype(BF16)
    prob = jnp.sum(total[:, width:], axis=1, keepdims=True)
    prob_ref[...] = jnp.sum(jnp.where(sel.astype(F32) > 0.5, prob, 0.0), axis=0, keepdims=True)


def place(shares, sel):
    rows = sel.shape[1]
    width = shares[0].shape[1] - LANES
    return call(
        place_body,
        "place",
        [struct((rows, width)), struct((1, rows), F32)],
        [IN_VMEM] * (len(shares) + 1),
        2 * LOC_CAP * rows * width,
        4 * rows * width,
    )(*shares, sel)


def split_cores(core_ref, mine_ref, theirs_ref, cols, block):
    part = mine_ref.shape[0]
    turned = block.T

    @pl.when(core_ref[0] == 0)
    def _():
        mine_ref[:, cols] = turned[:part]
        theirs_ref[:, cols] = turned[part:]

    @pl.when(core_ref[0] == 1)
    def _():
        mine_ref[:, cols] = turned[part:]
        theirs_ref[:, cols] = turned[:part]


def turn_x_body(core_ref, *refs):
    slices, (mine_ref, theirs_ref) = refs[:-2], refs[-2:]
    rows = slices[0].shape[0]
    for key, block in enumerate(slices):
        split_cores(core_ref, mine_ref, theirs_ref, slice(key * rows, (key + 1) * rows), block[...])


def turn_x(core, slices):
    rows, wide = slices[0].shape
    depth = rows * len(slices)
    return call(
        turn_x_body,
        "turn_x",
        [struct((wide // 2, depth))] * 2,
        [IN_SMEM] + [IN_VMEM] * len(slices),
        0,
        4 * depth * wide,
    )(core, *slices)


def turn_dy_body(chips, core_ref, *refs):
    slices, (mine_ref, theirs_ref) = refs[:-2], refs[-2:]
    rows = len(slices) * LOC_CAP
    for key in range(chips):
        span = slice(key * LOC_CAP, (key + 1) * LOC_CAP)
        block = jnp.concatenate([ref[span, :] for ref in slices], axis=0)
        split_cores(core_ref, mine_ref, theirs_ref, slice(key * rows, (key + 1) * rows), block)


def turn_dy(core, slices, chips):
    wide = slices[0].shape[1]
    depth = len(slices) * slices[0].shape[0]
    return call(
        functools.partial(turn_dy_body, chips),
        "turn_dy",
        [struct((wide // 2, depth))] * 2,
        [IN_SMEM] + [IN_VMEM] * len(slices),
        0,
        4 * depth * wide,
    )(core, *slices)


def stacked(refs):
    return jnp.concatenate([ref[...] for ref in refs], axis=0)


def wide_specs(parts, block):
    return [pl.BlockSpec((part.shape[0], block), lambda j: (0, j)) for part in parts]


def kept(array):
    return pl.BlockSpec(array.shape, lambda j: (0, 0))


def theirs_body(left_ref, *refs):
    out_ref = refs[-1]
    depth = sum(ref.shape[0] for ref in refs[:-1])
    out_ref[...] = jnp.dot(
        left_ref[:, :depth], stacked(refs[:-1]), preferred_element_type=F32
    ).astype(BF16)


def theirs_sums(left, parts):
    units = parts[0].shape[1]
    block = min(4 * BLOCK, units)
    depth = sum(part.shape[0] for part in parts)
    return call(
        theirs_body,
        "theirs_sums",
        struct((left.shape[0], units)),
        [kept(left)] + wide_specs(parts, block),
        2 * left.shape[0] * depth * units,
        2 * (depth + left.shape[0]) * units,
        grid=(units // block,),
        out_specs=pl.BlockSpec((left.shape[0], block), lambda j: (0, j)),
        limit=24,
    )(left, *parts)


def down_body(inv, left_ref, got_ref, *refs):
    out_ref = refs[-1]
    total = jnp.dot(left_ref[...], stacked(refs[:-1]), preferred_element_type=F32)
    out_ref[...] = ((total + got_ref[...].astype(F32)) * inv).T.astype(BF16)


def down_sums(left, got, parts, inv):
    part, units = got.shape
    block = min(2 * BLOCK, units)
    return call(
        functools.partial(down_body, inv),
        "down_sums",
        struct((units, part)),
        [kept(left)] + wide_specs([got, *parts], block),
        2 * left.size * units,
        2 * (left.shape[1] + 2 * part) * units,
        grid=(units // block,),
        out_specs=pl.BlockSpec((block, part), lambda j: (j, 0)),
        limit=24,
    )(left, got, *parts)


def pair_body(inv, count, steps, left_ref, other_ref, *refs):
    parts, others, (gate_ref, up_ref) = refs[:count], refs[count:-2], refs[-2:]
    total = jnp.dot(left_ref[...], stacked(parts), preferred_element_type=F32)
    total = total + jnp.dot(other_ref[...], stacked(others), preferred_element_type=F32)
    total = (total * inv).astype(BF16)

    @pl.when(pl.program_id(0) < steps)
    def _():
        gate_ref[...] = total

    @pl.when(pl.program_id(0) >= steps)
    def _():
        up_ref[...] = total


def pair_sums(left, other, parts, others, inv):
    part = left.shape[0]
    units = parts[0].shape[1]
    block = min(2 * BLOCK, units // 2)
    steps = units // 2 // block
    return call(
        functools.partial(pair_body, inv, len(parts), steps),
        "pair_sums",
        [struct((part, units // 2))] * 2,
        [kept(left), kept(other)] + wide_specs([*parts, *others], block),
        4 * left.size * units,
        4 * (left.shape[1] + part) * units,
        grid=(2 * steps,),
        out_specs=[
            pl.BlockSpec((part, block), lambda j: (0, jnp.minimum(j, steps - 1))),
            pl.BlockSpec((part, block), lambda j: (0, jnp.maximum(j - steps, 0))),
        ],
        limit=24,
    )(left, other, *parts, *others)


def after(value, *earlier):
    return lax.optimization_barrier((value, *earlier))[0]


def shards(tokens, out_grad, route_ids, route_prob, w_gate, w_up, w_down):
    data_ways = lax.axis_size("dp")
    etp_ways = lax.axis_size("etp")
    chips = data_ways // 2
    me = lax.axis_index("dp")
    chip = lax.shift_right_logical(me, 1).reshape(1)
    core = lax.bitwise_and(me, 1).reshape(1)
    inv = 1.0 / data_ways

    x_pack, sel = pack_x(route_ids.T, route_prob.reshape(1, -1), tokens)
    x_blocks = [x_pack] + [shift(x_pack, step) for step in range(1, etp_ways)]
    dy_pack, *dy_parts = pack_dy(chip, sel, out_grad, chips)
    dy_parts = jnp.concatenate(
        [dy_parts[0]] + [exchange(dy_parts[key], 2 * key) for key in range(1, chips)], axis=0
    )
    x_blocks[0] = after(x_blocks[0], dy_parts)
    x_all, *x_parts = join_x(chip, x_blocks, chips)
    x_slices = [x_parts[0]] + [exchange(x_parts[key], 2 * key) for key in range(1, chips)]
    dy_pack = after(dy_pack, x_all)
    dy_blocks = [dy_pack] + [shift(dy_pack, step) for step in range(1, etp_ways)]
    scaled, hidden, silu, slope = forward(x_all, w_gate, w_up)
    scaled = chip_gather(scaled, chips)

    grad, prob = backward(dy_blocks, w_down, after(hidden, *x_slices[1:]), silu, slope)
    grads = sum(chip_gather(grad, chips), [])
    dy_parts = after(dy_parts, *dy_blocks[1:])
    dy_slices = [dy_parts] + [shift(dy_parts, step) for step in range(1, etp_ways)]

    scaled = sum(scaled, [])
    shares = token_shares(w_gate, w_up, grad, after(prob, *scaled[1:]), etp_ways)
    shares = [after(share, *dy_slices[1:]) for share in shares]
    shares = [shares[0]] + [shift(shares[step], -step) for step in range(1, etp_ways)]
    grad_tokens, grad_prob = place(shares, sel)

    mine, theirs = turn_dy(core, dy_slices, chips)
    theirs = after(theirs, *shares[1:])
    got = exchange(theirs_sums(theirs, scaled), 1)
    grad_down = down_sums(mine, got, scaled, inv)

    mine, theirs = turn_x(core, x_slices)
    others = [
        exchange(after(part, *shares[1:]) if part.shape == grad.shape else part, 1) for part in grads
    ]
    mine = after(mine, grad_down, grad_tokens)
    grad_gate, grad_up = pair_sums(mine, exchange(theirs, 1), grads, others, inv)
    return (grad_tokens, grad_prob.reshape(-1), grad_gate, grad_up, grad_down)


def solution(mesh):
    placed = (
        P(("dp", "etp"), None),
        P(("dp", "etp"), None),
        P(("dp", "etp"), None),
        P(("dp", "etp")),
        P(None, "etp"),
        P(None, "etp"),
        P("etp", None),
    )
    return jax.shard_map(
        shards,
        mesh=mesh,
        in_specs=placed,
        out_specs=(
            P(("dp", "etp"), None),
            P(("dp", "etp")),
            P("dp", "etp"),
            P("dp", "etp"),
            P("etp", "dp"),
        ),
        check_vma=False,
    )
```

```python
import functools

import jax
import jax.numpy as jnp
from jax import lax
from jax.experimental import pallas as pl
from jax.experimental.pallas import tpu as pltpu
from jax.sharding import PartitionSpec as P

LOC_CAP = 32
LANES = 128
BLOCK = 256
MIB = 1024 * 1024
BF16 = jnp.bfloat16
F32 = jnp.float32
IN_VMEM = pl.BlockSpec(memory_space=pltpu.VMEM)
IN_HBM = pl.BlockSpec(memory_space=pltpu.HBM)
IN_SMEM = pl.BlockSpec(memory_space=pltpu.SMEM)


def call(body, name, out_shape, in_specs, flops, moved, scratch=(), limit=12, **kwargs):
    if "out_specs" not in kwargs:
        kwargs["out_specs"] = jax.tree.map(lambda _: IN_VMEM, out_shape)
    return pl.pallas_call(
        body,
        out_shape=out_shape,
        in_specs=in_specs,
        scratch_shapes=scratch,
        compiler_params=pltpu.CompilerParams(vmem_limit_bytes=limit * MIB),
        cost_estimate=pl.CostEstimate(
            flops=int(flops), bytes_accessed=int(moved), transcendentals=0
        ),
        name=name,
        **kwargs,
    )


def struct(shape, kind=BF16):
    return jax.ShapeDtypeStruct(shape, kind)


def nt_dot(left, right):
    return lax.dot_general(left, right, (((1,), (1,)), ((), ())), preferred_element_type=F32)


def shift(block, step):
    ways = lax.axis_size("etp")
    return lax.ppermute(block, "etp", [(i, (i + step) % ways) for i in range(ways)])


def exchange(block, bits):
    ways = lax.axis_size("dp")
    return lax.ppermute(block, "dp", [(i, i ^ bits) for i in range(ways)])


def chip_gather(piece, chips, turned):
    bits = [1 << k for k in range(chips.bit_length() - 1)]
    held = {0: piece}
    for bit in bits[::-1] if turned else bits:
        for key in sorted(held):
            held[key ^ bit] = exchange(held[key], 2 * bit)
    return [held[key] for key in range(chips)]


def pack_x_body(ids_ref, prob_ref, tokens_ref, x_ref, sel_ref):
    rows, width = tokens_ref.shape
    ids = ids_ref[...]
    routed = jnp.logical_or(ids[0:1] == 0, ids[1:2] == 0)
    flags = jnp.broadcast_to(routed.astype(F32), (8, rows)).astype(BF16)
    upto = (
        lax.broadcasted_iota(jnp.int32, (rows, rows), 0)
        <= lax.broadcasted_iota(jnp.int32, (rows, rows), 1)
    ).astype(F32).astype(BF16)
    slot = jnp.dot(flags, upto, preferred_element_type=F32)[0:1].astype(jnp.int32) - 1
    slots = lax.broadcasted_iota(jnp.int32, (LOC_CAP, rows), 0)
    matches = jnp.logical_and(slots == slot, routed)
    sel = matches.astype(F32)
    weight = jnp.sum(sel * prob_ref[...].astype(F32), axis=1, keepdims=True)
    sel = sel.astype(BF16)
    sel_ref[...] = sel
    x_ref[:, :width] = jnp.dot(sel, tokens_ref[...], preferred_element_type=F32).astype(BF16)
    x_ref[:, width:] = jnp.broadcast_to(weight, (LOC_CAP, LANES)).astype(BF16)


def pack_x(ids, prob, tokens):
    rows, width = tokens.shape
    return call(
        pack_x_body,
        "pack_x",
        [struct((LOC_CAP, width + LANES)), struct((LOC_CAP, rows))],
        [IN_VMEM] * 3,
        2 * LOC_CAP * rows * width,
        2 * rows * width,
    )(ids, prob, tokens)


def pack_dy_body(chips, chip_ref, sel_ref, grad_ref, dy_ref, *slice_refs):
    dy_ref[...] = jnp.dot(sel_ref[...], grad_ref[...], preferred_element_type=F32).astype(BF16)
    part = slice_refs[0].shape[1]
    for key in range(chips):
        first = pl.multiple_of((chip_ref[0] ^ key) * part, LANES)
        slice_refs[key][...] = dy_ref[:, pl.ds(first, part)]


def pack_dy(chip, sel, out_grad, chips):
    rows, width = out_grad.shape
    return call(
        functools.partial(pack_dy_body, chips),
        "pack_dy",
        [struct((LOC_CAP, width))] + [struct((LOC_CAP, width // chips))] * chips,
        [IN_SMEM] + [IN_VMEM] * 2,
        2 * LOC_CAP * rows * width,
        2 * rows * width,
    )(chip, sel, out_grad)


def join_x_body(chips, count, chip_ref, *refs):
    blocks, x_ref, slice_refs = refs[:count], refs[count], refs[count + 1 :]
    part = slice_refs[0].shape[1]
    for at, block in enumerate(blocks):
        x_ref[at * LOC_CAP : (at + 1) * LOC_CAP, :] = block[...]
    for key in range(chips):
        first = pl.multiple_of((chip_ref[0] ^ key) * part, LANES)
        slice_refs[key][...] = x_ref[:, pl.ds(first, part)]


def join_x(chip, blocks, chips):
    count = len(blocks)
    wide = blocks[0].shape[1]
    rows = count * LOC_CAP
    part = (wide - LANES) // chips
    return call(
        functools.partial(join_x_body, chips, count),
        "join_x",
        [struct((rows, wide))] + [struct((rows, part))] * chips,
        [IN_SMEM] + [IN_VMEM] * count,
        0,
        4 * rows * wide,
    )(chip, *blocks)


def windowed(groups, sems, ahead):
    made, at = [], 0
    for group in groups:
        made.append(
            [pltpu.make_async_copy(src, dst, sems.at[at + k]) for k, (src, dst) in enumerate(group)]
        )
        at += len(group)
    for copies in made[:ahead]:
        for copy in copies:
            copy.start()
    for step, copies in enumerate(made):
        for copy in copies:
            copy.wait()
        if step + ahead < len(made):
            for copy in made[step + ahead]:
                copy.start()
        yield step


def forward_body(
    half, x_ref, gate_hbm, up_hbm, scaled_ref, hidden_ref, silu_ref, slope_ref, gate_ref, up_ref, sems
):
    width, units = gate_hbm.shape
    x = x_ref[:, :width]
    weight = x_ref[:, width : width + 1].astype(F32)
    part = units // 2
    block = min(BLOCK, part)
    groups = []
    for at in range(0, part, block):
        src, dst = pl.ds(half * part + at, block), pl.ds(at, block)
        groups.append(
            [(gate_hbm.at[:, src], gate_ref.at[:, dst]), (up_hbm.at[:, src], up_ref.at[:, dst])]
        )
    for step in windowed(groups, sems, 4):
        cols = slice(step * block, (step + 1) * block)
        gate = jnp.dot(x, gate_ref[:, cols], preferred_element_type=F32)
        up = jnp.dot(x, up_ref[:, cols], preferred_element_type=F32)
        sig = 1.0 / (1.0 + jnp.exp(-gate))
        act = gate * sig
        hidden = (act * up).astype(BF16)
        hidden_ref[:, cols] = hidden
        scaled_ref[:, cols] = (weight * hidden.astype(F32)).astype(BF16)
        silu_ref[:, cols] = weight * act
        slope_ref[:, cols] = weight * up * sig * (1.0 + gate * (1.0 - sig))


def forward(x_all, w_gate, w_up, half):
    rows = x_all.shape[0]
    width, units = w_gate.shape
    part = units // 2
    return call(
        functools.partial(forward_body, half),
        "forward",
        [struct((rows, part), kind) for kind in (BF16, BF16, F32, F32)],
        [IN_VMEM] + [IN_HBM] * 2,
        4 * rows * width * part,
        4 * width * part,
        [pltpu.VMEM((width, part), BF16)] * 2
        + [pltpu.SemaphoreType.DMA((2 * (part // min(BLOCK, part)),))],
        limit=50,
    )(x_all, w_gate, w_up)


def backward_body(half, count, *refs):
    blocks = refs[:count]
    down_hbm, hidden_ref, silu_ref, slope_ref, grad_ref, prob_ref, down_ref, sems = refs[count:]
    rows, part = hidden_ref.shape
    block = min(BLOCK, part)
    groups = [
        [(down_hbm.at[pl.ds(half * part + at, block)], down_ref.at[pl.ds(at, block)])]
        for at in range(0, part, block)
    ]
    dy = jnp.concatenate([ref[...] for ref in blocks], axis=0)
    prob = jnp.zeros((rows, 1), F32)
    for step in windowed(groups, sems, 4):
        at = step * block
        cols = slice(at, at + block)
        raw = nt_dot(dy, down_ref[cols, :])
        grad_ref[:, cols] = (raw * slope_ref[:, cols]).astype(BF16)
        grad_ref[:, part + at : part + at + block] = (raw * silu_ref[:, cols]).astype(BF16)
        prob = prob + jnp.sum(hidden_ref[:, cols].astype(F32) * raw, axis=1, keepdims=True)
    prob_ref[...] = prob


def backward(dy_blocks, w_down, hidden, silu, slope, half):
    count = len(dy_blocks)
    rows, part = hidden.shape
    width = w_down.shape[1]
    return call(
        functools.partial(backward_body, half, count),
        "backward",
        [struct((rows, 2 * part)), struct((rows, 1), F32)],
        [IN_VMEM] * count + [IN_HBM] + [IN_VMEM] * 3,
        2 * rows * width * part,
        2 * width * part + 12 * rows * part,
        [pltpu.VMEM((part, width), BF16), pltpu.SemaphoreType.DMA((part // min(BLOCK, part),))],
        limit=50,
    )(*dy_blocks, w_down, hidden, silu, slope)


def token_body(count, gate_hbm, up_hbm, grad_a, grad_b, prob_a, prob_b, *refs):
    outs = refs[:count]
    gate_w, up_w, sems = refs[count:]
    width, units = gate_hbm.shape
    spans = [pl.ds(at, BLOCK) for at in range(0, width, BLOCK)]
    groups = [
        [(gate_hbm.at[span], gate_w.at[span]), (up_hbm.at[span], up_w.at[span])] for span in spans
    ]
    prob = prob_a[...] + prob_b[...]
    high = prob.astype(BF16).astype(F32)
    mid = (prob - high).astype(BF16).astype(F32)
    low = prob - high - mid
    lane = lax.broadcasted_iota(jnp.int32, (prob.shape[0], LANES), 1)
    terms = jnp.where(
        lane == 0, high, jnp.where(lane == 1, mid, jnp.where(lane == 2, low, 0.0))
    ).astype(BF16)
    for z in range(count):
        outs[z][:, width:] = terms[z * LOC_CAP : (z + 1) * LOC_CAP]
    part = units // 2
    gate = jnp.concatenate([grad_a[:, :part], grad_b[:, :part]], axis=1)
    up = jnp.concatenate([grad_a[:, part:], grad_b[:, part:]], axis=1)
    for step in windowed(groups, sems, 4):
        cols = slice(step * BLOCK, (step + 1) * BLOCK)
        share = (nt_dot(gate, gate_w[cols, :]) + nt_dot(up, up_w[cols, :])).astype(BF16)
        for z in range(count):
            outs[z][:, cols] = share[z * LOC_CAP : (z + 1) * LOC_CAP]


def token_shares(w_gate, w_up, grads, probs, count):
    width, units = w_gate.shape
    rows = count * LOC_CAP
    return call(
        functools.partial(token_body, count),
        "token_shares",
        [struct((LOC_CAP, width + LANES))] * count,
        [IN_HBM] * 2 + [IN_VMEM] * 4,
        4 * rows * width * units,
        4 * width * units,
        [pltpu.VMEM(w_gate.shape, BF16)] * 2 + [pltpu.SemaphoreType.DMA((2 * (width // BLOCK),))],
        limit=54,
    )(w_gate, w_up, *grads, *probs)


def place_body(*refs):
    shares, sel_ref, tokens_ref, prob_ref = refs[:-3], refs[-3], refs[-2], refs[-1]
    width = tokens_ref.shape[1]
    total = shares[0][...].astype(F32)
    for share in shares[1:]:
        total = total + share[...].astype(F32)
    rows = total[:, :width].astype(BF16)
    sel = sel_ref[...]
    tokens_ref[...] = lax.dot_general(
        sel, rows, (((0,), (0,)), ((), ())), preferred_element_type=F32
    ).astype(BF16)
    prob = jnp.sum(total[:, width:], axis=1, keepdims=True)
    prob_ref[...] = jnp.sum(jnp.where(sel.astype(F32) > 0.5, prob, 0.0), axis=0, keepdims=True)


def place(shares, sel):
    rows = sel.shape[1]
    width = shares[0].shape[1] - LANES
    return call(
        place_body,
        "place",
        [struct((rows, width)), struct((1, rows), F32)],
        [IN_VMEM] * (len(shares) + 1),
        2 * LOC_CAP * rows * width,
        4 * rows * width,
    )(*shares, sel)


def split_cores(core_ref, mine_ref, theirs_ref, cols, block):
    part = mine_ref.shape[0]
    turned = block.T

    @pl.when(core_ref[0] == 0)
    def _():
        mine_ref[:, cols] = turned[:part]
        theirs_ref[:, cols] = turned[part:]

    @pl.when(core_ref[0] == 1)
    def _():
        mine_ref[:, cols] = turned[part:]
        theirs_ref[:, cols] = turned[:part]


def turn_x_body(core_ref, *refs):
    slices, (mine_ref, theirs_ref) = refs[:-2], refs[-2:]
    rows = slices[0].shape[0]
    for key, block in enumerate(slices):
        split_cores(core_ref, mine_ref, theirs_ref, slice(key * rows, (key + 1) * rows), block[...])


def turn_x(core, slices):
    rows, wide = slices[0].shape
    depth = rows * len(slices)
    return call(
        turn_x_body,
        "turn_x",
        [struct((wide // 2, depth))] * 2,
        [IN_SMEM] + [IN_VMEM] * len(slices),
        0,
        4 * depth * wide,
    )(core, *slices)


def turn_dy_body(chips, core_ref, *refs):
    slices, (mine_ref, theirs_ref) = refs[:-2], refs[-2:]
    rows = len(slices) * LOC_CAP
    for key in range(chips):
        span = slice(key * LOC_CAP, (key + 1) * LOC_CAP)
        block = jnp.concatenate([ref[span, :] for ref in slices], axis=0)
        split_cores(core_ref, mine_ref, theirs_ref, slice(key * rows, (key + 1) * rows), block)


def turn_dy(core, slices, chips):
    wide = slices[0].shape[1]
    depth = len(slices) * slices[0].shape[0]
    return call(
        functools.partial(turn_dy_body, chips),
        "turn_dy",
        [struct((wide // 2, depth))] * 2,
        [IN_SMEM] + [IN_VMEM] * len(slices),
        0,
        4 * depth * wide,
    )(core, *slices)


def stacked(refs):
    return jnp.concatenate([ref[...] for ref in refs], axis=0)


def wide_specs(parts, block):
    return [pl.BlockSpec((part.shape[0], block), lambda j: (0, j)) for part in parts]


def kept(array):
    return pl.BlockSpec(array.shape, lambda j: (0, 0))


def half_specs(parts, block, steps, half):
    at = (lambda j: jnp.minimum(j, steps - 1)) if half == 0 else (lambda j: jnp.maximum(j - steps, 0))
    return [pl.BlockSpec((part.shape[0], block), lambda j: (0, at(j))) for part in parts]


def theirs_body(chips, steps, left_ref, *refs):
    out_ref = refs[-1]
    step = pl.program_id(0)
    for mine, parts in ((step < steps, refs[:chips]), (step >= steps, refs[chips:-1])):

        @pl.when(mine)
        def _():
            out_ref[...] = jnp.dot(
                left_ref[...], stacked(parts), preferred_element_type=F32
            ).astype(BF16)


def theirs_sums(left, parts_a, parts_b):
    part, depth = left.shape
    units = parts_a[0].shape[1]
    block = min(2 * BLOCK, units)
    steps = units // block
    return call(
        functools.partial(theirs_body, len(parts_a), steps),
        "theirs_sums",
        struct((part, 2 * units)),
        [kept(left)] + half_specs(parts_a, block, steps, 0) + half_specs(parts_b, block, steps, 1),
        4 * part * depth * units,
        4 * (depth + part) * units,
        grid=(2 * steps,),
        out_specs=pl.BlockSpec((part, block), lambda j: (0, j)),
        limit=24,
    )(left, *parts_a, *parts_b)


def down_body(inv, chips, steps, left_ref, got_ref, *refs):
    out_ref = refs[-1]
    step = pl.program_id(0)
    for mine, parts in ((step < steps, refs[:chips]), (step >= steps, refs[chips:-1])):

        @pl.when(mine)
        def _():
            total = jnp.dot(left_ref[...], stacked(parts), preferred_element_type=F32)
            out_ref[...] = ((total + got_ref[...].astype(F32)) * inv).T.astype(BF16)


def down_sums(left, got, parts_a, parts_b, inv):
    part, depth = left.shape
    units = parts_a[0].shape[1]
    block = min(2 * BLOCK, units)
    steps = units // block
    return call(
        functools.partial(down_body, inv, len(parts_a), steps),
        "down_sums",
        struct((2 * units, part)),
        [kept(left), pl.BlockSpec((part, block), lambda j: (0, j))]
        + half_specs(parts_a, block, steps, 0)
        + half_specs(parts_b, block, steps, 1),
        4 * part * depth * units,
        4 * (depth + 2 * part) * units,
        grid=(2 * steps,),
        out_specs=pl.BlockSpec((block, part), lambda j: (j, 0)),
        limit=24,
    )(left, got, *parts_a, *parts_b)


def pair_body(inv, chips, steps, left_ref, other_ref, *refs):
    parts, others, (gate_ref, up_ref) = refs[:chips], refs[chips : 2 * chips], refs[-2:]
    total = jnp.dot(left_ref[...], stacked(parts), preferred_element_type=F32)
    total = total + jnp.dot(other_ref[...], stacked(others), preferred_element_type=F32)
    total = (total * inv).astype(BF16)

    @pl.when(pl.program_id(0) < steps)
    def _():
        gate_ref[...] = total

    @pl.when(pl.program_id(0) >= steps)
    def _():
        up_ref[...] = total


def pair_sums(left, other, parts, others, earlier, half, inv):
    part, depth = left.shape
    units = parts[0].shape[1] // 2
    block = min(2 * BLOCK, units)
    steps = units // block
    held = list(earlier)
    count = 2 + 2 * len(parts)
    return call(
        functools.partial(pair_body, inv, len(parts), steps),
        "pair_sums",
        [struct((part, 2 * units))] * 2,
        [kept(left), kept(other)]
        + wide_specs([*parts, *others], block)
        + [pl.BlockSpec(memory_space=pl.ANY)] * len(held),
        8 * part * depth * units,
        8 * (depth + part) * units,
        grid=(2 * steps,),
        out_specs=[
            pl.BlockSpec((part, block), lambda j: (0, half * steps + jnp.minimum(j, steps - 1))),
            pl.BlockSpec((part, block), lambda j: (0, half * steps + jnp.maximum(j - steps, 0))),
        ],
        input_output_aliases={count: 0, count + 1: 1} if held else {},
        limit=24,
    )(left, other, *parts, *others, *held)


def after(value, *earlier):
    return lax.optimization_barrier((value, *earlier))[0]


def shards(tokens, out_grad, route_ids, route_prob, w_gate, w_up, w_down):
    data_ways = lax.axis_size("dp")
    etp_ways = lax.axis_size("etp")
    chips = data_ways // 2
    me = lax.axis_index("dp")
    chip = lax.shift_right_logical(me, 1).reshape(1)
    core = lax.bitwise_and(me, 1).reshape(1)
    inv = 1.0 / data_ways

    x_pack, sel = pack_x(route_ids.T, route_prob.reshape(1, -1), tokens)
    x_blocks = [x_pack] + [shift(x_pack, step) for step in range(1, etp_ways)]
    dy_pack, *dy_parts = pack_dy(chip, sel, out_grad, chips)
    dy_parts = jnp.concatenate(
        [dy_parts[0]] + [exchange(dy_parts[key], 2 * key) for key in range(1, chips)], axis=0
    )
    dy_pack = after(dy_pack, dy_parts)
    dy_blocks = [dy_pack] + [shift(dy_pack, step) for step in range(1, etp_ways)]
    x_all, *x_parts = join_x(chip, x_blocks, chips)
    x_slices = [x_parts[0]] + [exchange(x_parts[key], 2 * key) for key in range(1, chips)]
    near = [x_slices[1 << k] for k in range(chips.bit_length() - 1)]
    inputs = (x_all, after(x_all, *near, *dy_blocks[1:-1]))
    scaled, grads, probs, kept_halves = [], [], [], []
    for half in range(2):
        piece, *rest = forward(inputs[half], w_gate, w_up, half)
        scaled.append(chip_gather(piece, chips, half == 1))
        kept_halves.append(rest)
    for half in range(2):
        hidden, silu, slope = kept_halves[half]
        grad, prob = backward(dy_blocks, w_down, after(hidden, *x_slices[1:]), silu, slope, half)
        grads.append(grad)
        probs.append(prob)
    parts = [chip_gather(grads[half], chips, half == 1) for half in range(2)]
    dy_parts = after(dy_parts, *dy_blocks[1:])
    dy_slices = [dy_parts] + [shift(dy_parts, step) for step in range(1, etp_ways)]

    probs[0] = after(probs[0], *scaled[0][1:], *scaled[1][1:], *dy_slices[1:])
    shares = token_shares(w_gate, w_up, grads, probs, etp_ways)
    shares = [shares[0]] + [shift(shares[step], -step) for step in range(1, etp_ways)]
    grad_tokens, grad_prob = place(shares, sel)

    mine, theirs = turn_dy(core, dy_slices, chips)
    theirs = after(theirs, probs[1])
    got = exchange(theirs_sums(theirs, *scaled), 1)
    grad_down = down_sums(mine, got, *scaled, inv)

    mine, theirs = turn_x(core, x_slices)
    mine = after(mine, grad_down, grad_tokens)
    far = exchange(theirs, 1)
    held = ()
    for half in range(2):
        others = [
            exchange(after(part, parts[0][-1]) if key.bit_count() == 1 else part, 1)
            for key, part in enumerate(parts[half])
        ]
        held = pair_sums(mine, far, parts[half], others, held, half, inv)
    grad_gate, grad_up = held
    return (grad_tokens, grad_prob.reshape(-1), grad_gate, grad_up, grad_down)


def solution(mesh):
    placed = (
        P(("dp", "etp"), None),
        P(("dp", "etp"), None),
        P(("dp", "etp"), None),
        P(("dp", "etp")),
        P(None, "etp"),
        P(None, "etp"),
        P("etp", None),
    )
    return jax.shard_map(
        shards,
        mesh=mesh,
        in_specs=placed,
        out_specs=(
            P(("dp", "etp"), None),
            P(("dp", "etp")),
            P("dp", "etp"),
            P("dp", "etp"),
            P("etp", "dp"),
        ),
        check_vma=False,
    )
```

```python
import functools

import jax
import jax.numpy as jnp
from jax import lax
from jax.experimental import pallas as pl
from jax.experimental.pallas import tpu as pltpu
from jax.sharding import PartitionSpec as P

LOC_CAP = 32
LANES = 128
BLOCK = 256
MIB = 1024 * 1024
BF16 = jnp.bfloat16
F32 = jnp.float32
IN_VMEM = pl.BlockSpec(memory_space=pltpu.VMEM)
IN_HBM = pl.BlockSpec(memory_space=pltpu.HBM)
IN_SMEM = pl.BlockSpec(memory_space=pltpu.SMEM)


def call(body, name, out_shape, in_specs, flops, moved, scratch=(), limit=12, **kwargs):
    if "out_specs" not in kwargs:
        kwargs["out_specs"] = jax.tree.map(lambda _: IN_VMEM, out_shape)
    return pl.pallas_call(
        body,
        out_shape=out_shape,
        in_specs=in_specs,
        scratch_shapes=scratch,
        compiler_params=pltpu.CompilerParams(vmem_limit_bytes=limit * MIB),
        cost_estimate=pl.CostEstimate(
            flops=int(flops), bytes_accessed=int(moved), transcendentals=0
        ),
        name=name,
        **kwargs,
    )


def struct(shape, kind=BF16):
    return jax.ShapeDtypeStruct(shape, kind)


def nt_dot(left, right):
    return lax.dot_general(left, right, (((1,), (1,)), ((), ())), preferred_element_type=F32)


def shift(block, step):
    ways = lax.axis_size("etp")
    return lax.ppermute(block, "etp", [(i, (i + step) % ways) for i in range(ways)])


def exchange(block, bits):
    ways = lax.axis_size("dp")
    return lax.ppermute(block, "dp", [(i, i ^ bits) for i in range(ways)])


def chip_gather(piece, chips, turned):
    bits = [1 << k for k in range(chips.bit_length() - 1)]
    held = {0: piece}
    for bit in bits[::-1] if turned else bits:
        for key in sorted(held):
            held[key ^ bit] = exchange(held[key], 2 * bit)
    return [held[key] for key in range(chips)]


def pack_x_body(ids_ref, prob_ref, tokens_ref, x_ref, sel_ref):
    rows, width = tokens_ref.shape
    ids = ids_ref[...]
    routed = jnp.logical_or(ids[0:1] == 0, ids[1:2] == 0)
    flags = jnp.broadcast_to(routed.astype(F32), (8, rows)).astype(BF16)
    upto = (
        lax.broadcasted_iota(jnp.int32, (rows, rows), 0)
        <= lax.broadcasted_iota(jnp.int32, (rows, rows), 1)
    ).astype(F32).astype(BF16)
    slot = jnp.dot(flags, upto, preferred_element_type=F32)[0:1].astype(jnp.int32) - 1
    slots = lax.broadcasted_iota(jnp.int32, (LOC_CAP, rows), 0)
    matches = jnp.logical_and(slots == slot, routed)
    sel = matches.astype(F32)
    weight = jnp.sum(sel * prob_ref[...].astype(F32), axis=1, keepdims=True)
    sel = sel.astype(BF16)
    sel_ref[...] = sel
    x_ref[:, :width] = jnp.dot(sel, tokens_ref[...], preferred_element_type=F32).astype(BF16)
    x_ref[:, width:] = jnp.broadcast_to(weight, (LOC_CAP, LANES)).astype(BF16)


def pack_x(ids, prob, tokens):
    rows, width = tokens.shape
    return call(
        pack_x_body,
        "pack_x",
        [struct((LOC_CAP, width + LANES)), struct((LOC_CAP, rows))],
        [IN_VMEM] * 3,
        2 * LOC_CAP * rows * width,
        2 * rows * width,
    )(ids, prob, tokens)


def pack_dy_body(chips, chip_ref, sel_ref, grad_ref, dy_ref, *slice_refs):
    dy_ref[...] = jnp.dot(sel_ref[...], grad_ref[...], preferred_element_type=F32).astype(BF16)
    part = slice_refs[0].shape[1]
    for key in range(chips):
        first = pl.multiple_of((chip_ref[0] ^ key) * part, LANES)
        slice_refs[key][...] = dy_ref[:, pl.ds(first, part)]


def pack_dy(chip, sel, out_grad, chips):
    rows, width = out_grad.shape
    return call(
        functools.partial(pack_dy_body, chips),
        "pack_dy",
        [struct((LOC_CAP, width))] + [struct((LOC_CAP, width // chips))] * chips,
        [IN_SMEM] + [IN_VMEM] * 2,
        2 * LOC_CAP * rows * width,
        2 * rows * width,
    )(chip, sel, out_grad)


def join_x_body(chips, count, chip_ref, *refs):
    blocks, x_ref, slice_refs = refs[:count], refs[count], refs[count + 1 :]
    part = slice_refs[0].shape[1]
    for at, block in enumerate(blocks):
        x_ref[at * LOC_CAP : (at + 1) * LOC_CAP, :] = block[...]
    for key in range(chips):
        first = pl.multiple_of((chip_ref[0] ^ key) * part, LANES)
        slice_refs[key][...] = x_ref[:, pl.ds(first, part)]


def join_x(chip, blocks, chips):
    count = len(blocks)
    wide = blocks[0].shape[1]
    rows = count * LOC_CAP
    part = (wide - LANES) // chips
    return call(
        functools.partial(join_x_body, chips, count),
        "join_x",
        [struct((rows, wide))] + [struct((rows, part))] * chips,
        [IN_SMEM] + [IN_VMEM] * count,
        0,
        4 * rows * wide,
    )(chip, *blocks)


def windowed(groups, sems, ahead):
    made, at = [], 0
    for group in groups:
        made.append(
            [pltpu.make_async_copy(src, dst, sems.at[at + k]) for k, (src, dst) in enumerate(group)]
        )
        at += len(group)
    for copies in made[:ahead]:
        for copy in copies:
            copy.start()
    for step, copies in enumerate(made):
        for copy in copies:
            copy.wait()
        if step + ahead < len(made):
            for copy in made[step + ahead]:
                copy.start()
        yield step


def forward_body(
    half, x_ref, gate_hbm, up_hbm, scaled_ref, hidden_ref, silu_ref, slope_ref, gate_ref, up_ref, sems
):
    width, units = gate_hbm.shape
    x = x_ref[:, :width]
    weight = x_ref[:, width : width + 1].astype(F32)
    part = units // 2
    block = min(BLOCK, part)
    groups = []
    for at in range(0, part, block):
        src, dst = pl.ds(half * part + at, block), pl.ds(at, block)
        groups.append(
            [(gate_hbm.at[:, src], gate_ref.at[:, dst]), (up_hbm.at[:, src], up_ref.at[:, dst])]
        )
    for step in windowed(groups, sems, 4):
        cols = slice(step * block, (step + 1) * block)
        gate = jnp.dot(x, gate_ref[:, cols], preferred_element_type=F32)
        up = jnp.dot(x, up_ref[:, cols], preferred_element_type=F32)
        sig = 1.0 / (1.0 + jnp.exp(-gate))
        act = gate * sig
        hidden = (act * up).astype(BF16)
        hidden_ref[:, cols] = hidden
        scaled_ref[:, cols] = (weight * hidden.astype(F32)).astype(BF16)
        silu_ref[:, cols] = weight * act
        slope_ref[:, cols] = weight * up * sig * (1.0 + gate * (1.0 - sig))


def forward(x_all, w_gate, w_up, half):
    rows = x_all.shape[0]
    width, units = w_gate.shape
    part = units // 2
    return call(
        functools.partial(forward_body, half),
        "forward",
        [struct((rows, part), kind) for kind in (BF16, BF16, F32, F32)],
        [IN_VMEM] + [IN_HBM] * 2,
        4 * rows * width * part,
        4 * width * part,
        [pltpu.VMEM((width, part), BF16)] * 2
        + [pltpu.SemaphoreType.DMA((2 * (part // min(BLOCK, part)),))],
        limit=50,
    )(x_all, w_gate, w_up)


def backward_body(half, count, *refs):
    blocks = refs[:count]
    down_hbm, hidden_ref, silu_ref, slope_ref, grad_ref, prob_ref = refs[count : count + 6]
    down_ref, raw_ref, sems = refs[count + 6 :]
    part = hidden_ref.shape[1]
    rows, width = pl.ds(half * part, part), down_hbm.shape[1]
    block = 2 * BLOCK
    spans = [pl.ds(at, block) for at in range(0, width, block)]
    groups = [[(down_hbm.at[rows, span], down_ref.at[:, span])] for span in spans]
    for step in windowed(groups, sems, 4):
        cols = slice(step * block, (step + 1) * block)
        dy = jnp.concatenate([ref[:, cols] for ref in blocks], axis=0)
        raw = nt_dot(dy, down_ref[:, cols])
        raw_ref[...] = raw if step == 0 else raw_ref[...] + raw
    raw = raw_ref[...]
    grad_ref[:, :part] = (raw * slope_ref[...]).astype(BF16)
    grad_ref[:, part:] = (raw * silu_ref[...]).astype(BF16)
    prob_ref[...] = jnp.sum(hidden_ref[...].astype(F32) * raw, axis=1, keepdims=True)


def backward(dy_blocks, w_down, hidden, silu, slope, half):
    count = len(dy_blocks)
    rows, part = hidden.shape
    width = w_down.shape[1]
    return call(
        functools.partial(backward_body, half, count),
        "backward",
        [struct((rows, 2 * part)), struct((rows, 1), F32)],
        [IN_VMEM] * count + [IN_HBM] + [IN_VMEM] * 3,
        2 * rows * width * part,
        2 * width * part + 12 * rows * part,
        [
            pltpu.VMEM((part, width), BF16),
            pltpu.VMEM((rows, part), F32),
            pltpu.SemaphoreType.DMA((width // (2 * BLOCK),)),
        ],
        limit=50,
    )(*dy_blocks, w_down, hidden, silu, slope)


def token_body(half, count, gate_hbm, up_hbm, grad_ref, *refs):
    gate_w, up_w, sems = refs[-3:]
    width, units = gate_hbm.shape
    part = units // 2
    block = min(BLOCK, part)
    groups = []
    for at in range(0, part, block):
        src, dst = pl.ds(half * part + at, block), pl.ds(at, block)
        groups.append(
            [(gate_hbm.at[:, src], gate_w.at[:, dst]), (up_hbm.at[:, src], up_w.at[:, dst])]
        )
    total_ref = refs[0] if half == 0 else refs[-4]
    for step in windowed(groups, sems, 4):
        at = step * block
        cols = slice(at, at + block)
        share = nt_dot(grad_ref[:, cols], gate_w[:, cols])
        share = share + nt_dot(grad_ref[:, part + at : part + at + block], up_w[:, cols])
        total_ref[...] = share if step == 0 else total_ref[...] + share
    if half == 0:
        return
    earlier_ref, prob_a, prob_b = refs[:3]
    outs = refs[3 : 3 + count]
    prob = prob_a[...] + prob_b[...]
    high = prob.astype(BF16).astype(F32)
    mid = (prob - high).astype(BF16).astype(F32)
    low = prob - high - mid
    lane = lax.broadcasted_iota(jnp.int32, (prob.shape[0], LANES), 1)
    terms = jnp.where(
        lane == 0, high, jnp.where(lane == 1, mid, jnp.where(lane == 2, low, 0.0))
    ).astype(BF16)
    for z in range(count):
        rows = slice(z * LOC_CAP, (z + 1) * LOC_CAP)
        outs[z][:, :width] = (total_ref[rows, :] + earlier_ref[rows, :]).astype(BF16)
        outs[z][:, width:] = terms[rows]


def token_sums(w_gate, w_up, grad, half, earlier, count):
    width, units = w_gate.shape
    part = units // 2
    rows = count * LOC_CAP
    weights = [pltpu.VMEM((width, part), BF16)] * 2
    total = [] if half == 0 else [pltpu.VMEM((rows, width), F32)]
    return call(
        functools.partial(token_body, half, count),
        "token_sums",
        struct((rows, width), F32) if half == 0 else [struct((LOC_CAP, width + LANES))] * count,
        [IN_HBM] * 2 + [IN_VMEM] * (1 + len(earlier)),
        4 * rows * width * part,
        4 * width * part,
        total + weights + [pltpu.SemaphoreType.DMA((2 * (part // min(BLOCK, part)),))],
        limit=50,
    )(w_gate, w_up, grad, *earlier)


def place_body(*refs):
    shares, sel_ref, tokens_ref, prob_ref = refs[:-3], refs[-3], refs[-2], refs[-1]
    width = tokens_ref.shape[1]
    total = shares[0][...].astype(F32)
    for share in shares[1:]:
        total = total + share[...].astype(F32)
    rows = total[:, :width].astype(BF16)
    sel = sel_ref[...]
    tokens_ref[...] = lax.dot_general(
        sel, rows, (((0,), (0,)), ((), ())), preferred_element_type=F32
    ).astype(BF16)
    prob = jnp.sum(total[:, width:], axis=1, keepdims=True)
    prob_ref[...] = jnp.sum(jnp.where(sel.astype(F32) > 0.5, prob, 0.0), axis=0, keepdims=True)


def place(shares, sel):
    rows = sel.shape[1]
    width = shares[0].shape[1] - LANES
    return call(
        place_body,
        "place",
        [struct((rows, width)), struct((1, rows), F32)],
        [IN_VMEM] * (len(shares) + 1),
        2 * LOC_CAP * rows * width,
        4 * rows * width,
    )(*shares, sel)


def split_cores(core_ref, mine_ref, theirs_ref, cols, block):
    part = mine_ref.shape[0]
    turned = block.T

    @pl.when(core_ref[0] == 0)
    def _():
        mine_ref[:, cols] = turned[:part]
        theirs_ref[:, cols] = turned[part:]

    @pl.when(core_ref[0] == 1)
    def _():
        mine_ref[:, cols] = turned[part:]
        theirs_ref[:, cols] = turned[:part]


def turn_x_body(core_ref, *refs):
    slices, (mine_ref, theirs_ref) = refs[:-2], refs[-2:]
    rows = slices[0].shape[0]
    for key, block in enumerate(slices):
        split_cores(core_ref, mine_ref, theirs_ref, slice(key * rows, (key + 1) * rows), block[...])


def turn_x(core, slices):
    rows, wide = slices[0].shape
    depth = rows * len(slices)
    return call(
        turn_x_body,
        "turn_x",
        [struct((wide // 2, depth))] * 2,
        [IN_SMEM] + [IN_VMEM] * len(slices),
        0,
        4 * depth * wide,
    )(core, *slices)


def turn_dy_body(chips, core_ref, *refs):
    slices, (mine_ref, theirs_ref) = refs[:-2], refs[-2:]
    rows = len(slices) * LOC_CAP
    for key in range(chips):
        span = slice(key * LOC_CAP, (key + 1) * LOC_CAP)
        block = jnp.concatenate([ref[span, :] for ref in slices], axis=0)
        split_cores(core_ref, mine_ref, theirs_ref, slice(key * rows, (key + 1) * rows), block)


def turn_dy(core, slices, chips):
    wide = slices[0].shape[1]
    depth = len(slices) * slices[0].shape[0]
    return call(
        functools.partial(turn_dy_body, chips),
        "turn_dy",
        [struct((wide // 2, depth))] * 2,
        [IN_SMEM] + [IN_VMEM] * len(slices),
        0,
        4 * depth * wide,
    )(core, *slices)


def stacked(refs):
    return jnp.concatenate([ref[...] for ref in refs], axis=0)


def wide_specs(parts, block):
    return [pl.BlockSpec((part.shape[0], block), lambda j: (0, j)) for part in parts]


def kept(array):
    return pl.BlockSpec(array.shape, lambda j: (0, 0))


def half_specs(parts, block, steps, half):
    at = (lambda j: jnp.minimum(j, steps - 1)) if half == 0 else (lambda j: jnp.maximum(j - steps, 0))
    return [pl.BlockSpec((part.shape[0], block), lambda j: (0, at(j))) for part in parts]


def theirs_body(chips, steps, left_ref, *refs):
    out_ref = refs[-1]
    step = pl.program_id(0)
    for mine, parts in ((step < steps, refs[:chips]), (step >= steps, refs[chips:-1])):

        @pl.when(mine)
        def _():
            out_ref[...] = jnp.dot(
                left_ref[...], stacked(parts), preferred_element_type=F32
            ).astype(BF16)


def theirs_sums(left, parts_a, parts_b):
    part, depth = left.shape
    units = parts_a[0].shape[1]
    block = min(2 * BLOCK, units)
    steps = units // block
    return call(
        functools.partial(theirs_body, len(parts_a), steps),
        "theirs_sums",
        struct((part, 2 * units)),
        [kept(left)] + half_specs(parts_a, block, steps, 0) + half_specs(parts_b, block, steps, 1),
        4 * part * depth * units,
        4 * (depth + part) * units,
        grid=(2 * steps,),
        out_specs=pl.BlockSpec((part, block), lambda j: (0, j)),
        limit=24,
    )(left, *parts_a, *parts_b)


def down_body(inv, chips, steps, left_ref, got_ref, *refs):
    out_ref = refs[-1]
    step = pl.program_id(0)
    for mine, parts in ((step < steps, refs[:chips]), (step >= steps, refs[chips:-1])):

        @pl.when(mine)
        def _():
            total = jnp.dot(left_ref[...], stacked(parts), preferred_element_type=F32)
            out_ref[...] = ((total + got_ref[...].astype(F32)) * inv).T.astype(BF16)


def down_sums(left, got, parts_a, parts_b, inv):
    part, depth = left.shape
    units = parts_a[0].shape[1]
    block = min(2 * BLOCK, units)
    steps = units // block
    return call(
        functools.partial(down_body, inv, len(parts_a), steps),
        "down_sums",
        struct((2 * units, part)),
        [kept(left), pl.BlockSpec((part, block), lambda j: (0, j))]
        + half_specs(parts_a, block, steps, 0)
        + half_specs(parts_b, block, steps, 1),
        4 * part * depth * units,
        4 * (depth + 2 * part) * units,
        grid=(2 * steps,),
        out_specs=pl.BlockSpec((block, part), lambda j: (j, 0)),
        limit=24,
    )(left, got, *parts_a, *parts_b)


def pair_body(inv, chips, steps, left_ref, other_ref, *refs):
    parts, others, (gate_ref, up_ref) = refs[:chips], refs[chips : 2 * chips], refs[-2:]
    total = jnp.dot(left_ref[...], stacked(parts), preferred_element_type=F32)
    total = total + jnp.dot(other_ref[...], stacked(others), preferred_element_type=F32)
    total = (total * inv).astype(BF16)

    @pl.when(pl.program_id(0) < steps)
    def _():
        gate_ref[...] = total

    @pl.when(pl.program_id(0) >= steps)
    def _():
        up_ref[...] = total


def pair_sums(left, other, parts, others, earlier, half, inv):
    part, depth = left.shape
    units = parts[0].shape[1] // 2
    block = min(2 * BLOCK, units)
    steps = units // block
    held = list(earlier)
    count = 2 + 2 * len(parts)
    return call(
        functools.partial(pair_body, inv, len(parts), steps),
        "pair_sums",
        [struct((part, 2 * units))] * 2,
        [kept(left), kept(other)]
        + wide_specs([*parts, *others], block)
        + [pl.BlockSpec(memory_space=pl.ANY)] * len(held),
        8 * part * depth * units,
        8 * (depth + part) * units,
        grid=(2 * steps,),
        out_specs=[
            pl.BlockSpec((part, block), lambda j: (0, half * steps + jnp.minimum(j, steps - 1))),
            pl.BlockSpec((part, block), lambda j: (0, half * steps + jnp.maximum(j - steps, 0))),
        ],
        input_output_aliases={count: 0, count + 1: 1} if held else {},
        limit=24,
    )(left, other, *parts, *others, *held)


def after(value, *earlier):
    return lax.optimization_barrier((value, *earlier))[0]


def shards(tokens, out_grad, route_ids, route_prob, w_gate, w_up, w_down):
    data_ways = lax.axis_size("dp")
    etp_ways = lax.axis_size("etp")
    chips = data_ways // 2
    me = lax.axis_index("dp")
    chip = lax.shift_right_logical(me, 1).reshape(1)
    core = lax.bitwise_and(me, 1).reshape(1)
    inv = 1.0 / data_ways

    x_pack, sel = pack_x(route_ids.T, route_prob.reshape(1, -1), tokens)
    x_blocks = [x_pack] + [shift(x_pack, step) for step in range(1, etp_ways)]
    dy_pack, *dy_parts = pack_dy(chip, sel, out_grad, chips)
    dy_parts = jnp.concatenate(
        [dy_parts[0]] + [exchange(dy_parts[key], 2 * key) for key in range(1, chips)], axis=0
    )
    x_blocks[0] = after(x_blocks[0], dy_parts)
    x_all, *x_parts = join_x(chip, x_blocks, chips)
    x_slices = [x_parts[0]] + [exchange(x_parts[key], 2 * key) for key in range(1, chips)]
    dy_pack = after(dy_pack, x_all)
    dy_blocks = [dy_pack] + [shift(dy_pack, step) for step in range(1, etp_ways)]
    near = [x_slices[1 << k] for k in range(chips.bit_length() - 1)]
    inputs = (x_all, after(x_all, *near, *dy_blocks[1:-1]))
    scaled, grads, probs, kept_halves = [], [], [], []
    for half in range(2):
        piece, *rest = forward(inputs[half], w_gate, w_up, half)
        scaled.append(chip_gather(piece, chips, half == 1))
        kept_halves.append(rest)
    earlier = list(x_slices[1:])
    later = []
    for key in range(1, chips):
        (earlier if key.bit_count() == 1 else later).extend((scaled[0][key], scaled[1][key]))
    for half in range(2):
        hidden, silu, slope = kept_halves[half]
        hidden = after(hidden, *earlier)
        grad, prob = backward(dy_blocks, w_down, hidden, silu, slope, half)
        grads.append(grad)
        probs.append(prob)
        if half == 0:
            first = token_sums(w_gate, w_up, grad, 0, (), etp_ways)
            earlier = [*later, first]
    parts = [chip_gather(grads[half], chips, half == 1) for half in range(2)]
    dy_parts = after(dy_parts, probs[1])
    dy_slices = [dy_parts] + [shift(dy_parts, step) for step in range(1, etp_ways)]

    shares = token_sums(w_gate, w_up, grads[1], 1, (first, *probs), etp_ways)
    shares = [after(share, *dy_slices[1:]) for share in shares]
    shares = [shares[0]] + [shift(shares[step], -step) for step in range(1, etp_ways)]
    grad_tokens, grad_prob = place(shares, sel)

    mine, theirs = turn_dy(core, dy_slices, chips)
    got = exchange(theirs_sums(theirs, *scaled), 1)
    grad_down = down_sums(mine, got, *scaled, inv)

    mine, theirs = turn_x(core, x_slices)
    far = exchange(theirs, 1)
    held = ()
    for half in range(2):
        others = [
            exchange(after(part, parts[0][-1]) if key.bit_count() < 2 else part, 1)
            for key, part in enumerate(parts[half])
        ]
        if half == 1:
            mine = after(mine, grad_down)
        held = pair_sums(mine, far, parts[half], others, held, half, inv)
    grad_gate, grad_up = held
    return (grad_tokens, grad_prob.reshape(-1), grad_gate, grad_up, grad_down)


def solution(mesh):
    placed = (
        P(("dp", "etp"), None),
        P(("dp", "etp"), None),
        P(("dp", "etp"), None),
        P(("dp", "etp")),
        P(None, "etp"),
        P(None, "etp"),
        P("etp", None),
    )
    return jax.shard_map(
        shards,
        mesh=mesh,
        in_specs=placed,
        out_specs=(
            P(("dp", "etp"), None),
            P(("dp", "etp")),
            P("dp", "etp"),
            P("dp", "etp"),
            P("etp", "dp"),
        ),
        check_vma=False,
    )
```

```python
import functools

import jax
import jax.numpy as jnp
from jax import lax
from jax.experimental import pallas as pl
from jax.experimental.pallas import tpu as pltpu
from jax.sharding import PartitionSpec as P

LOC_CAP = 32
LANES = 128
BLOCK = 256
MIB = 1024 * 1024
BF16 = jnp.bfloat16
F32 = jnp.float32
IN_VMEM = pl.BlockSpec(memory_space=pltpu.VMEM)
IN_HBM = pl.BlockSpec(memory_space=pltpu.HBM)
IN_SMEM = pl.BlockSpec(memory_space=pltpu.SMEM)


def call(body, name, out_shape, in_specs, flops, moved, scratch=(), limit=12, **kwargs):
    if "out_specs" not in kwargs:
        kwargs["out_specs"] = jax.tree.map(lambda _: IN_VMEM, out_shape)
    return pl.pallas_call(
        body,
        out_shape=out_shape,
        in_specs=in_specs,
        scratch_shapes=scratch,
        compiler_params=pltpu.CompilerParams(vmem_limit_bytes=limit * MIB),
        cost_estimate=pl.CostEstimate(
            flops=int(flops), bytes_accessed=int(moved), transcendentals=0
        ),
        name=name,
        **kwargs,
    )


def whole(shape):
    return pl.BlockSpec(shape, lambda *_: (0,) * len(shape))


def struct(shape, kind=BF16):
    return jax.ShapeDtypeStruct(shape, kind)


def nt_dot(left, right):
    return lax.dot_general(left, right, (((1,), (1,)), ((), ())), preferred_element_type=F32)


def shift(block, step):
    ways = lax.axis_size("etp")
    return lax.ppermute(block, "etp", [(i, (i + step) % ways) for i in range(ways)])


def exchange(block, bits):
    ways = lax.axis_size("dp")
    return lax.ppermute(block, "dp", [(i, i ^ bits) for i in range(ways)])


def chip_gather(piece, chips, turned):
    bits = [1 << k for k in range(chips.bit_length() - 1)]
    held = {0: piece}
    for bit in bits[::-1] if turned else bits:
        for key in sorted(held):
            held[key ^ bit] = exchange(held[key], 2 * bit)
    return [held[key] for key in range(chips)]


def pack_x_body(ids_ref, prob_ref, tokens_ref, x_ref, sel_ref):
    rows, width = tokens_ref.shape
    ids = ids_ref[...]
    routed = jnp.logical_or(ids[0:1] == 0, ids[1:2] == 0)
    flags = jnp.broadcast_to(routed.astype(F32), (8, rows)).astype(BF16)
    upto = (
        lax.broadcasted_iota(jnp.int32, (rows, rows), 0)
        <= lax.broadcasted_iota(jnp.int32, (rows, rows), 1)
    ).astype(F32).astype(BF16)
    slot = jnp.dot(flags, upto, preferred_element_type=F32)[0:1].astype(jnp.int32) - 1
    slots = lax.broadcasted_iota(jnp.int32, (LOC_CAP, rows), 0)
    matches = jnp.logical_and(slots == slot, routed)
    sel = matches.astype(F32)
    weight = jnp.sum(sel * prob_ref[...].astype(F32), axis=1, keepdims=True)
    sel = sel.astype(BF16)
    sel_ref[...] = sel
    x_ref[:, :width] = jnp.dot(sel, tokens_ref[...], preferred_element_type=F32).astype(BF16)
    x_ref[:, width:] = jnp.broadcast_to(weight, (LOC_CAP, LANES)).astype(BF16)


def pack_x(ids, prob, tokens):
    rows, width = tokens.shape
    return call(
        pack_x_body,
        "pack_x",
        [struct((LOC_CAP, width + LANES)), struct((LOC_CAP, rows))],
        [IN_VMEM] * 3,
        2 * LOC_CAP * rows * width,
        2 * rows * width,
    )(ids, prob, tokens)


def pack_dy_body(sel_ref, grad_ref, dy_ref):
    dy_ref[...] = jnp.dot(sel_ref[...], grad_ref[...], preferred_element_type=F32).astype(BF16)


def pack_dy(sel, out_grad):
    rows, width = out_grad.shape
    return call(
        pack_dy_body,
        "pack_dy",
        struct((LOC_CAP, width)),
        [IN_VMEM] * 2,
        2 * LOC_CAP * rows * width,
        2 * rows * width,
    )(sel, out_grad)


def slice_body(chips, count, chip_ref, *refs):
    outs = refs[count:]
    wide = outs[0].shape[1]
    for key in range(chips):
        at = pl.multiple_of((chip_ref[0] ^ key) * wide, LANES)
        for z in range(count):
            outs[key][z * LOC_CAP : (z + 1) * LOC_CAP, :] = refs[z][:, pl.ds(at, wide)]


def slices_of(chip, blocks, width, chips):
    count = len(blocks)
    rows = count * LOC_CAP
    return call(
        functools.partial(slice_body, chips, count),
        "slices",
        [struct((rows, width // chips))] * chips,
        [IN_SMEM] + [IN_VMEM] * count,
        0,
        4 * rows * width,
    )(chip, *blocks)


def windowed(groups, sems, ahead):
    made, at = [], 0
    for group in groups:
        made.append(
            [pltpu.make_async_copy(src, dst, sems.at[at + k]) for k, (src, dst) in enumerate(group)]
        )
        at += len(group)
    for copies in made[:ahead]:
        for copy in copies:
            copy.start()
    for step, copies in enumerate(made):
        for copy in copies:
            copy.wait()
        if step + ahead < len(made):
            for copy in made[step + ahead]:
                copy.start()
        yield step


def forward_body(half, count, *refs):
    blocks = refs[:count]
    gate_hbm, up_hbm, scaled_ref, hidden_ref, silu_ref, slope_ref = refs[count : count + 6]
    gate_ref, up_ref, sems = refs[count + 6 :]
    width, units = gate_hbm.shape
    part = units // 2
    block = min(BLOCK, part)
    groups = []
    for at in range(0, part, block):
        src, dst = pl.ds(half * part + at, block), pl.ds(at, block)
        groups.append(
            [(gate_hbm.at[:, src], gate_ref.at[:, dst]), (up_hbm.at[:, src], up_ref.at[:, dst])]
        )
    x = jnp.concatenate([ref[:, :width] for ref in blocks], axis=0)
    weight = jnp.concatenate([ref[:, width : width + 1] for ref in blocks], axis=0).astype(F32)
    for step in windowed(groups, sems, 4):
        cols = slice(step * block, (step + 1) * block)
        gate = jnp.dot(x, gate_ref[:, cols], preferred_element_type=F32)
        up = jnp.dot(x, up_ref[:, cols], preferred_element_type=F32)
        sig = 1.0 / (1.0 + jnp.exp(-gate))
        act = gate * sig
        hidden = (act * up).astype(BF16)
        hidden_ref[:, cols] = hidden
        scaled_ref[:, cols] = (weight * hidden.astype(F32)).astype(BF16)
        silu_ref[:, cols] = weight * act
        slope_ref[:, cols] = weight * up * sig * (1.0 + gate * (1.0 - sig))


def forward(x_blocks, w_gate, w_up, half):
    count = len(x_blocks)
    rows = count * LOC_CAP
    width, units = w_gate.shape
    part = units // 2
    return call(
        functools.partial(forward_body, half, count),
        "forward",
        [struct((rows, part), kind) for kind in (BF16, BF16, F32, F32)],
        [IN_VMEM] * count + [IN_HBM] * 2,
        4 * rows * width * part,
        4 * width * part,
        [pltpu.VMEM((width, part), BF16)] * 2
        + [pltpu.SemaphoreType.DMA((2 * (part // min(BLOCK, part)),))],
        limit=50,
    )(*x_blocks, w_gate, w_up)


def backward_body(half, count, *refs):
    blocks = refs[:count]
    down_hbm, hidden_hbm, silu_hbm, slope_hbm, grad_ref, prob_ref = refs[count : count + 6]
    down_ref, raw_ref, hidden_ref, silu_ref, slope_ref, sems, late_sems = refs[count + 6 :]
    part = hidden_ref.shape[1]
    late = [
        pltpu.make_async_copy(src, dst, late_sems.at[at])
        for at, (src, dst) in enumerate(
            ((hidden_hbm, hidden_ref), (silu_hbm, silu_ref), (slope_hbm, slope_ref))
        )
    ]
    for copy in late:
        copy.start()
    rows, width = pl.ds(half * part, part), down_hbm.shape[1]
    block = 2 * BLOCK
    spans = [pl.ds(at, block) for at in range(0, width, block)]
    groups = [[(down_hbm.at[rows, span], down_ref.at[:, span])] for span in spans]
    for step in windowed(groups, sems, 4):
        cols = slice(step * block, (step + 1) * block)
        dy = jnp.concatenate([ref[:, cols] for ref in blocks], axis=0)
        raw = nt_dot(dy, down_ref[:, cols])
        raw_ref[...] = raw if step == 0 else raw_ref[...] + raw
    for copy in late:
        copy.wait()
    raw = raw_ref[...]
    grad_ref[:, :part] = (raw * slope_ref[...]).astype(BF16)
    grad_ref[:, part:] = (raw * silu_ref[...]).astype(BF16)
    prob_ref[...] = jnp.sum(hidden_ref[...].astype(F32) * raw, axis=1, keepdims=True)


def backward(dy_blocks, w_down, hidden, silu, slope, half):
    count = len(dy_blocks)
    rows, part = hidden.shape
    width = w_down.shape[1]
    return call(
        functools.partial(backward_body, half, count),
        "backward",
        [struct((rows, 2 * part)), struct((rows, 1), F32)],
        [IN_VMEM] * count + [IN_HBM] + [pl.BlockSpec(memory_space=pl.ANY)] * 3,
        2 * rows * width * part,
        2 * width * part + 12 * rows * part,
        [
            pltpu.VMEM((part, width), BF16),
            pltpu.VMEM((rows, part), F32),
            pltpu.VMEM((rows, part), BF16),
            pltpu.VMEM((rows, part), F32),
            pltpu.VMEM((rows, part), F32),
            pltpu.SemaphoreType.DMA((width // (2 * BLOCK),)),
            pltpu.SemaphoreType.DMA((3,)),
        ],
        limit=50,
    )(*dy_blocks, w_down, hidden, silu, slope)


def token_body(half, count, gate_hbm, up_hbm, grad_ref, *refs):
    gate_w, up_w, sems = refs[-3:]
    width, units = gate_hbm.shape
    part = units // 2
    block = min(BLOCK, part)
    groups = []
    for at in range(0, part, block):
        src, dst = pl.ds(half * part + at, block), pl.ds(at, block)
        groups.append(
            [(gate_hbm.at[:, src], gate_w.at[:, dst]), (up_hbm.at[:, src], up_w.at[:, dst])]
        )
    total_ref = refs[0] if half == 0 else refs[-4]
    for step in windowed(groups, sems, 4):
        at = step * block
        cols = slice(at, at + block)
        share = nt_dot(grad_ref[:, cols], gate_w[:, cols])
        share = share + nt_dot(grad_ref[:, part + at : part + at + block], up_w[:, cols])
        total_ref[...] = share if step == 0 else total_ref[...] + share
    if half == 0:
        return
    earlier_ref, prob_a, prob_b = refs[:3]
    outs = refs[3 : 3 + count]
    prob = prob_a[...] + prob_b[...]
    high = prob.astype(BF16).astype(F32)
    mid = (prob - high).astype(BF16).astype(F32)
    low = prob - high - mid
    lane = lax.broadcasted_iota(jnp.int32, (prob.shape[0], LANES), 1)
    terms = jnp.where(
        lane == 0, high, jnp.where(lane == 1, mid, jnp.where(lane == 2, low, 0.0))
    ).astype(BF16)
    for z in range(count):
        rows = slice(z * LOC_CAP, (z + 1) * LOC_CAP)
        outs[z][:, :width] = (total_ref[rows, :] + earlier_ref[rows, :]).astype(BF16)
        outs[z][:, width:] = terms[rows]


def token_sums(w_gate, w_up, grad, half, earlier, count):
    width, units = w_gate.shape
    part = units // 2
    rows = count * LOC_CAP
    weights = [pltpu.VMEM((width, part), BF16)] * 2
    total = [] if half == 0 else [pltpu.VMEM((rows, width), F32)]
    return call(
        functools.partial(token_body, half, count),
        "token_sums",
        struct((rows, width), F32) if half == 0 else [struct((LOC_CAP, width + LANES))] * count,
        [IN_HBM] * 2 + [IN_VMEM] * (1 + len(earlier)),
        4 * rows * width * part,
        4 * width * part,
        total + weights + [pltpu.SemaphoreType.DMA((2 * (part // min(BLOCK, part)),))],
        limit=50,
    )(w_gate, w_up, grad, *earlier)


def place_body(*refs):
    shares, sel_ref, tokens_ref, prob_ref = refs[:-3], refs[-3], refs[-2], refs[-1]
    width = tokens_ref.shape[1]
    total = shares[0][...].astype(F32)
    for share in shares[1:]:
        total = total + share[...].astype(F32)
    rows = total[:, :width].astype(BF16)
    sel = sel_ref[...]
    tokens_ref[...] = lax.dot_general(
        sel, rows, (((0,), (0,)), ((), ())), preferred_element_type=F32
    ).astype(BF16)
    prob = jnp.sum(total[:, width:], axis=1, keepdims=True)
    prob_ref[...] = jnp.sum(jnp.where(sel.astype(F32) > 0.5, prob, 0.0), axis=0, keepdims=True)


def place(shares, sel):
    rows = sel.shape[1]
    width = shares[0].shape[1] - LANES
    return call(
        place_body,
        "place",
        [struct((rows, width)), struct((1, rows), F32)],
        [IN_VMEM] * (len(shares) + 1),
        2 * LOC_CAP * rows * width,
        4 * rows * width,
    )(*shares, sel)


def split_cores(core_ref, mine_ref, theirs_ref, cols, block):
    part = mine_ref.shape[0]
    turned = block.T

    @pl.when(core_ref[0] == 0)
    def _():
        mine_ref[:, cols] = turned[:part]
        theirs_ref[:, cols] = turned[part:]

    @pl.when(core_ref[0] == 1)
    def _():
        mine_ref[:, cols] = turned[part:]
        theirs_ref[:, cols] = turned[:part]


def turn_body(core_ref, *refs):
    slices, (mine_ref, theirs_ref) = refs[:-2], refs[-2:]
    rows = slices[0].shape[0]
    for key, ref in enumerate(slices):
        cols = slice(key * rows, (key + 1) * rows)
        split_cores(core_ref, mine_ref, theirs_ref, cols, ref[...])


def turn(core, slices):
    rows, wide = slices[0].shape
    depth = rows * len(slices)
    out = (wide // 2, depth)
    return call(
        turn_body,
        "turn",
        [struct(out)] * 2,
        [IN_SMEM] + [whole(slices[0].shape)] * len(slices),
        0,
        4 * depth * wide,
        grid=(1,),
        out_specs=[whole(out)] * 2,
    )(core, *slices)


def stacked(refs):
    return jnp.concatenate([ref[...] for ref in refs], axis=0)


def wide_specs(parts, block):
    return [pl.BlockSpec((part.shape[0], block), lambda j: (0, j)) for part in parts]


def kept(array):
    return pl.BlockSpec(array.shape, lambda j: (0, 0))


def half_specs(parts, block, steps, half):
    at = (lambda j: jnp.minimum(j, steps - 1)) if half == 0 else (lambda j: jnp.maximum(j - steps, 0))
    return [pl.BlockSpec((part.shape[0], block), lambda j: (0, at(j))) for part in parts]


def theirs_body(chips, steps, left_ref, *refs):
    out_ref = refs[-1]
    step = pl.program_id(0)
    for mine, parts in ((step < steps, refs[:chips]), (step >= steps, refs[chips:-1])):

        @pl.when(mine)
        def _():
            out_ref[...] = jnp.dot(
                left_ref[...], stacked(parts), preferred_element_type=F32
            ).astype(BF16)


def theirs_sums(left, parts_a, parts_b):
    part, depth = left.shape
    units = parts_a[0].shape[1]
    block = min(2 * BLOCK, units)
    steps = units // block
    return call(
        functools.partial(theirs_body, len(parts_a), steps),
        "theirs_sums",
        struct((part, 2 * units)),
        [kept(left)] + half_specs(parts_a, block, steps, 0) + half_specs(parts_b, block, steps, 1),
        4 * part * depth * units,
        4 * (depth + part) * units,
        grid=(2 * steps,),
        out_specs=pl.BlockSpec((part, block), lambda j: (0, j)),
        limit=24,
    )(left, *parts_a, *parts_b)


def down_body(inv, chips, steps, left_ref, got_ref, *refs):
    out_ref = refs[-1]
    step = pl.program_id(0)
    for mine, parts in ((step < steps, refs[:chips]), (step >= steps, refs[chips:-1])):

        @pl.when(mine)
        def _():
            total = jnp.dot(left_ref[...], stacked(parts), preferred_element_type=F32)
            out_ref[...] = ((total + got_ref[...].astype(F32)) * inv).T.astype(BF16)


def down_sums(left, got, parts_a, parts_b, inv):
    part, depth = left.shape
    units = parts_a[0].shape[1]
    block = min(2 * BLOCK, units)
    steps = units // block
    return call(
        functools.partial(down_body, inv, len(parts_a), steps),
        "down_sums",
        struct((2 * units, part)),
        [kept(left), pl.BlockSpec((part, block), lambda j: (0, j))]
        + half_specs(parts_a, block, steps, 0)
        + half_specs(parts_b, block, steps, 1),
        4 * part * depth * units,
        4 * (depth + 2 * part) * units,
        grid=(2 * steps,),
        out_specs=pl.BlockSpec((block, part), lambda j: (j, 0)),
        limit=24,
    )(left, got, *parts_a, *parts_b)


def pair_body(inv, chips, steps, left_ref, other_ref, *refs):
    parts, others, (gate_ref, up_ref) = refs[:chips], refs[chips : 2 * chips], refs[-2:]
    total = jnp.dot(left_ref[...], stacked(parts), preferred_element_type=F32)
    total = total + jnp.dot(other_ref[...], stacked(others), preferred_element_type=F32)
    total = (total * inv).astype(BF16)

    @pl.when(pl.program_id(0) < steps)
    def _():
        gate_ref[...] = total

    @pl.when(pl.program_id(0) >= steps)
    def _():
        up_ref[...] = total


def pair_sums(left, other, parts, others, earlier, half, inv):
    part, depth = left.shape
    units = parts[0].shape[1] // 2
    block = min(2 * BLOCK, units)
    steps = units // block
    held = list(earlier)
    count = 2 + 2 * len(parts)
    return call(
        functools.partial(pair_body, inv, len(parts), steps),
        "pair_sums",
        [struct((part, 2 * units))] * 2,
        [kept(left), kept(other)]
        + wide_specs([*parts, *others], block)
        + [pl.BlockSpec(memory_space=pl.ANY)] * len(held),
        8 * part * depth * units,
        8 * (depth + part) * units,
        grid=(2 * steps,),
        out_specs=[
            pl.BlockSpec((part, block), lambda j: (0, half * steps + jnp.minimum(j, steps - 1))),
            pl.BlockSpec((part, block), lambda j: (0, half * steps + jnp.maximum(j - steps, 0))),
        ],
        input_output_aliases={count: 0, count + 1: 1} if held else {},
        limit=24,
    )(left, other, *parts, *others, *held)


def after(value, *earlier):
    return lax.optimization_barrier((value, *earlier))[0]


def shards(tokens, out_grad, route_ids, route_prob, w_gate, w_up, w_down):
    data_ways = lax.axis_size("dp")
    etp_ways = lax.axis_size("etp")
    chips = data_ways // 2
    me = lax.axis_index("dp")
    chip = lax.shift_right_logical(me, 1).reshape(1)
    core = lax.bitwise_and(me, 1).reshape(1)
    inv = 1.0 / data_ways

    x_pack, sel = pack_x(route_ids.T, route_prob.reshape(1, -1), tokens)
    x_blocks = [x_pack] + [shift(x_pack, step) for step in range(1, etp_ways)]
    dy_pack = after(pack_dy(sel, out_grad), *x_blocks[1:])
    dy_blocks = [dy_pack] + [shift(dy_pack, step) for step in range(1, etp_ways)]
    width = tokens.shape[1]
    x_slices = slices_of(chip, x_blocks, width, chips)
    x_slices = [x_slices[0]] + [exchange(x_slices[key], 2 * key) for key in range(1, chips)]
    near = [x_slices[1 << k] for k in range(chips.bit_length() - 1)]
    inputs = (x_blocks, [after(x_pack, *near, *dy_blocks[1:]), *x_blocks[1:]])
    scaled, grads, probs, kept_halves = [], [], [], []
    for half in range(2):
        piece, *rest = forward(inputs[half], w_gate, w_up, half)
        scaled.append(chip_gather(piece, chips, half == 1))
        kept_halves.append(rest)
    dy_slices = slices_of(chip, dy_blocks, width, chips)
    dy_slices = [dy_slices[0]] + [exchange(dy_slices[key], 2 * key) for key in range(1, chips)]
    earlier = [scaled[0][key] for key in range(chips) if key.bit_count() == 1]
    later = [*x_slices[1:], *dy_slices[1:], *scaled[0][1:], *scaled[1][1:]]
    for half in range(2):
        hidden, silu, slope = kept_halves[half]
        blocks = [after(dy_blocks[0], *earlier), *dy_blocks[1:]]
        grad, prob = backward(blocks, w_down, hidden, silu, slope, half)
        grads.append(grad)
        probs.append(prob)
        if half == 0:
            first = token_sums(w_gate, w_up, grad, 0, (), etp_ways)
            earlier = [*later, first]
    parts = [chip_gather(grads[half], chips, half == 1) for half in range(2)]

    shares = token_sums(w_gate, w_up, grads[1], 1, (first, *probs), etp_ways)
    sums_after = shares[0]
    shares = [shares[0]] + [shift(shares[step], -step) for step in range(1, etp_ways)]
    grad_tokens, grad_prob = place(shares, sel)

    x_mine, x_theirs = turn(core, x_slices)
    dy_mine, dy_theirs = turn(core, dy_slices)
    dy_theirs = after(dy_theirs, sums_after)
    got = exchange(theirs_sums(dy_theirs, *scaled), 1)
    grad_down = down_sums(dy_mine, got, *scaled, inv)

    far = exchange(after(x_theirs, sums_after), 1)
    held = ()
    for half in range(2):
        others = [
            exchange(after(part, parts[0][-1]) if key.bit_count() < 2 else part, 1)
            for key, part in enumerate(parts[half])
        ]
        if half == 1:
            x_mine = after(x_mine, grad_down)
        held = pair_sums(x_mine, far, parts[half], others, held, half, inv)
    grad_gate, grad_up = held
    return (grad_tokens, grad_prob.reshape(-1), grad_gate, grad_up, grad_down)


def solution(mesh):
    placed = (
        P(("dp", "etp"), None),
        P(("dp", "etp"), None),
        P(("dp", "etp"), None),
        P(("dp", "etp")),
        P(None, "etp"),
        P(None, "etp"),
        P("etp", None),
    )
    return jax.shard_map(
        shards,
        mesh=mesh,
        in_specs=placed,
        out_specs=(
            P(("dp", "etp"), None),
            P(("dp", "etp")),
            P("dp", "etp"),
            P("dp", "etp"),
            P("etp", "dp"),
        ),
        check_vma=False,
    )
```

```python
import functools

import jax
import jax.numpy as jnp
from jax import lax
from jax.experimental import pallas as pl
from jax.experimental.pallas import tpu as pltpu
from jax.sharding import PartitionSpec as P

LOC_CAP = 32
LANES = 128
BLOCK = 256
MIB = 1024 * 1024
BF16 = jnp.bfloat16
F32 = jnp.float32
IN_VMEM = pl.BlockSpec(memory_space=pltpu.VMEM)
IN_HBM = pl.BlockSpec(memory_space=pltpu.HBM)
IN_SMEM = pl.BlockSpec(memory_space=pltpu.SMEM)


def call(body, name, out_shape, in_specs, flops, moved, scratch=(), limit=12, **kwargs):
    if "out_specs" not in kwargs:
        kwargs["out_specs"] = jax.tree.map(lambda _: IN_VMEM, out_shape)
    return pl.pallas_call(
        body,
        out_shape=out_shape,
        in_specs=in_specs,
        scratch_shapes=scratch,
        compiler_params=pltpu.CompilerParams(vmem_limit_bytes=limit * MIB),
        cost_estimate=pl.CostEstimate(
            flops=int(flops), bytes_accessed=int(moved), transcendentals=0
        ),
        name=name,
        **kwargs,
    )


def whole(shape):
    return pl.BlockSpec(shape, lambda *_: (0,) * len(shape))


def struct(shape, kind=BF16):
    return jax.ShapeDtypeStruct(shape, kind)


def nt_dot(left, right):
    return lax.dot_general(left, right, (((1,), (1,)), ((), ())), preferred_element_type=F32)


def shift(block, step):
    ways = lax.axis_size("etp")
    return lax.ppermute(block, "etp", [(i, (i + step) % ways) for i in range(ways)])


def exchange(block, bits):
    ways = lax.axis_size("dp")
    return lax.ppermute(block, "dp", [(i, i ^ bits) for i in range(ways)])


def chip_gather(piece, chips, turned):
    bits = [1 << k for k in range(chips.bit_length() - 1)]
    held = {0: piece}
    for bit in bits[::-1] if turned else bits:
        for key in sorted(held):
            held[key ^ bit] = exchange(held[key], 2 * bit)
    return [held[key] for key in range(chips)]


def pack_x_body(ids_ref, prob_ref, tokens_ref, x_ref, sel_ref):
    rows, width = tokens_ref.shape
    ids = ids_ref[...]
    routed = jnp.logical_or(ids[0:1] == 0, ids[1:2] == 0)
    flags = jnp.broadcast_to(routed.astype(F32), (8, rows)).astype(BF16)
    upto = (
        lax.broadcasted_iota(jnp.int32, (rows, rows), 0)
        <= lax.broadcasted_iota(jnp.int32, (rows, rows), 1)
    ).astype(F32).astype(BF16)
    slot = jnp.dot(flags, upto, preferred_element_type=F32)[0:1].astype(jnp.int32) - 1
    slots = lax.broadcasted_iota(jnp.int32, (LOC_CAP, rows), 0)
    matches = jnp.logical_and(slots == slot, routed)
    sel = matches.astype(F32)
    weight = jnp.sum(sel * prob_ref[...].astype(F32), axis=1, keepdims=True)
    sel = sel.astype(BF16)
    sel_ref[...] = sel
    x_ref[:, :width] = jnp.dot(sel, tokens_ref[...], preferred_element_type=F32).astype(BF16)
    x_ref[:, width:] = jnp.broadcast_to(weight, (LOC_CAP, LANES)).astype(BF16)


def pack_x(ids, prob, tokens):
    rows, width = tokens.shape
    return call(
        pack_x_body,
        "pack_x",
        [struct((LOC_CAP, width + LANES)), struct((LOC_CAP, rows))],
        [IN_VMEM] * 3,
        2 * LOC_CAP * rows * width,
        2 * rows * width,
    )(ids, prob, tokens)


def pack_dy_body(sel_ref, grad_ref, dy_ref):
    dy_ref[...] = jnp.dot(sel_ref[...], grad_ref[...], preferred_element_type=F32).astype(BF16)


def pack_dy(sel, out_grad):
    rows, width = out_grad.shape
    return call(
        pack_dy_body,
        "pack_dy",
        struct((LOC_CAP, width)),
        [IN_VMEM] * 2,
        2 * LOC_CAP * rows * width,
        2 * rows * width,
    )(sel, out_grad)


def slice_body(chips, count, *refs):
    out_ref = refs[-1]
    wide = out_ref.shape[2] // 2
    for chip in range(chips):
        span = slice(chip * wide, (chip + 1) * wide)
        for z in range(count):
            rows = slice(z * LOC_CAP, (z + 1) * LOC_CAP)
            out_ref[chip, rows, :wide] = refs[z][:, span]
            out_ref[chip, rows, wide:] = refs[count + z][:, span]


def slices_of(x_blocks, dy_blocks, chips):
    count = len(x_blocks)
    rows = count * LOC_CAP
    width = dy_blocks[0].shape[1]
    return call(
        functools.partial(slice_body, chips, count),
        "slices",
        struct((chips, rows, 2 * width // chips)),
        [IN_VMEM] * (2 * count),
        0,
        8 * rows * width,
    )(*x_blocks, *dy_blocks)


def windowed(groups, sems, ahead):
    made, at = [], 0
    for group in groups:
        made.append(
            [pltpu.make_async_copy(src, dst, sems.at[at + k]) for k, (src, dst) in enumerate(group)]
        )
        at += len(group)
    for copies in made[:ahead]:
        for copy in copies:
            copy.start()
    for step, copies in enumerate(made):
        for copy in copies:
            copy.wait()
        if step + ahead < len(made):
            for copy in made[step + ahead]:
                copy.start()
        yield step


def forward_body(half, count, *refs):
    blocks = refs[:count]
    gate_hbm, up_hbm, scaled_ref, hidden_ref, silu_ref, slope_ref = refs[count : count + 6]
    gate_ref, up_ref, sems = refs[count + 6 :]
    width, units = gate_hbm.shape
    part = units // 2
    block = min(BLOCK, part)
    groups = []
    for at in range(0, part, block):
        src, dst = pl.ds(half * part + at, block), pl.ds(at, block)
        groups.append(
            [(gate_hbm.at[:, src], gate_ref.at[:, dst]), (up_hbm.at[:, src], up_ref.at[:, dst])]
        )
    x = jnp.concatenate([ref[:, :width] for ref in blocks], axis=0)
    weight = jnp.concatenate([ref[:, width : width + 1] for ref in blocks], axis=0).astype(F32)
    for step in windowed(groups, sems, 4):
        cols = slice(step * block, (step + 1) * block)
        gate = jnp.dot(x, gate_ref[:, cols], preferred_element_type=F32)
        up = jnp.dot(x, up_ref[:, cols], preferred_element_type=F32)
        sig = 1.0 / (1.0 + jnp.exp(-gate))
        act = gate * sig
        hidden = (act * up).astype(BF16)
        hidden_ref[:, cols] = hidden
        scaled_ref[:, cols] = (weight * hidden.astype(F32)).astype(BF16)
        silu_ref[:, cols] = weight * act
        slope_ref[:, cols] = weight * up * sig * (1.0 + gate * (1.0 - sig))


def forward(x_blocks, w_gate, w_up, half):
    count = len(x_blocks)
    rows = count * LOC_CAP
    width, units = w_gate.shape
    part = units // 2
    return call(
        functools.partial(forward_body, half, count),
        "forward",
        [struct((rows, part), kind) for kind in (BF16, BF16, F32, F32)],
        [IN_VMEM] * count + [IN_HBM] * 2,
        4 * rows * width * part,
        4 * width * part,
        [pltpu.VMEM((width, part), BF16)] * 2
        + [pltpu.SemaphoreType.DMA((2 * (part // min(BLOCK, part)),))],
        limit=50,
    )(*x_blocks, w_gate, w_up)


def backward_body(half, count, *refs):
    blocks = refs[:count]
    down_hbm, hidden_hbm, silu_hbm, slope_hbm, grad_ref, prob_ref = refs[count : count + 6]
    down_ref, raw_ref, hidden_ref, silu_ref, slope_ref, sems, late_sems = refs[count + 6 :]
    part = hidden_ref.shape[1]
    late = [
        pltpu.make_async_copy(src, dst, late_sems.at[at])
        for at, (src, dst) in enumerate(
            ((hidden_hbm, hidden_ref), (silu_hbm, silu_ref), (slope_hbm, slope_ref))
        )
    ]
    for copy in late:
        copy.start()
    rows, width = pl.ds(half * part, part), down_hbm.shape[1]
    block = 2 * BLOCK
    spans = [pl.ds(at, block) for at in range(0, width, block)]
    groups = [[(down_hbm.at[rows, span], down_ref.at[:, span])] for span in spans]
    for step in windowed(groups, sems, 4):
        cols = slice(step * block, (step + 1) * block)
        dy = jnp.concatenate([ref[:, cols] for ref in blocks], axis=0)
        raw = nt_dot(dy, down_ref[:, cols])
        raw_ref[...] = raw if step == 0 else raw_ref[...] + raw
    for copy in late:
        copy.wait()
    raw = raw_ref[...]
    grad_ref[:, :part] = (raw * slope_ref[...]).astype(BF16)
    grad_ref[:, part:] = (raw * silu_ref[...]).astype(BF16)
    prob_ref[...] = jnp.sum(hidden_ref[...].astype(F32) * raw, axis=1, keepdims=True)


def backward(dy_blocks, w_down, hidden, silu, slope, half):
    count = len(dy_blocks)
    rows, part = hidden.shape
    width = w_down.shape[1]
    return call(
        functools.partial(backward_body, half, count),
        "backward",
        [struct((rows, 2 * part)), struct((rows, 1), F32)],
        [IN_VMEM] * count + [IN_HBM] + [pl.BlockSpec(memory_space=pl.ANY)] * 3,
        2 * rows * width * part,
        2 * width * part + 12 * rows * part,
        [
            pltpu.VMEM((part, width), BF16),
            pltpu.VMEM((rows, part), F32),
            pltpu.VMEM((rows, part), BF16),
            pltpu.VMEM((rows, part), F32),
            pltpu.VMEM((rows, part), F32),
            pltpu.SemaphoreType.DMA((width // (2 * BLOCK),)),
            pltpu.SemaphoreType.DMA((3,)),
        ],
        limit=50,
    )(*dy_blocks, w_down, hidden, silu, slope)


def token_body(half, count, gate_hbm, up_hbm, grad_ref, *refs):
    gate_w, up_w, sems = refs[-3:]
    width, units = gate_hbm.shape
    part = units // 2
    block = min(BLOCK, part)
    groups = []
    for at in range(0, part, block):
        src, dst = pl.ds(half * part + at, block), pl.ds(at, block)
        groups.append(
            [(gate_hbm.at[:, src], gate_w.at[:, dst]), (up_hbm.at[:, src], up_w.at[:, dst])]
        )
    total_ref = refs[0] if half == 0 else refs[-4]
    for step in windowed(groups, sems, 4):
        at = step * block
        cols = slice(at, at + block)
        share = nt_dot(grad_ref[:, cols], gate_w[:, cols])
        share = share + nt_dot(grad_ref[:, part + at : part + at + block], up_w[:, cols])
        total_ref[...] = share if step == 0 else total_ref[...] + share
    if half == 0:
        return
    earlier_ref, prob_a, prob_b = refs[:3]
    outs = refs[3 : 3 + count]
    prob = prob_a[...] + prob_b[...]
    high = prob.astype(BF16).astype(F32)
    mid = (prob - high).astype(BF16).astype(F32)
    low = prob - high - mid
    lane = lax.broadcasted_iota(jnp.int32, (prob.shape[0], LANES), 1)
    terms = jnp.where(
        lane == 0, high, jnp.where(lane == 1, mid, jnp.where(lane == 2, low, 0.0))
    ).astype(BF16)
    for z in range(count):
        rows = slice(z * LOC_CAP, (z + 1) * LOC_CAP)
        outs[z][:, :width] = (total_ref[rows, :] + earlier_ref[rows, :]).astype(BF16)
        outs[z][:, width:] = terms[rows]


def token_sums(w_gate, w_up, grad, half, earlier, count):
    width, units = w_gate.shape
    part = units // 2
    rows = count * LOC_CAP
    weights = [pltpu.VMEM((width, part), BF16)] * 2
    total = [] if half == 0 else [pltpu.VMEM((rows, width), F32)]
    return call(
        functools.partial(token_body, half, count),
        "token_sums",
        struct((rows, width), F32) if half == 0 else [struct((LOC_CAP, width + LANES))] * count,
        [IN_HBM] * 2 + [IN_VMEM] * (1 + len(earlier)),
        4 * rows * width * part,
        4 * width * part,
        total + weights + [pltpu.SemaphoreType.DMA((2 * (part // min(BLOCK, part)),))],
        limit=50,
    )(w_gate, w_up, grad, *earlier)


def place_body(*refs):
    shares, sel_ref, tokens_ref, prob_ref = refs[:-3], refs[-3], refs[-2], refs[-1]
    width = tokens_ref.shape[1]
    total = shares[0][...].astype(F32)
    for share in shares[1:]:
        total = total + share[...].astype(F32)
    rows = total[:, :width].astype(BF16)
    sel = sel_ref[...]
    tokens_ref[...] = lax.dot_general(
        sel, rows, (((0,), (0,)), ((), ())), preferred_element_type=F32
    ).astype(BF16)
    prob = jnp.sum(total[:, width:], axis=1, keepdims=True)
    prob_ref[...] = jnp.sum(jnp.where(sel.astype(F32) > 0.5, prob, 0.0), axis=0, keepdims=True)


def place(shares, sel):
    rows = sel.shape[1]
    width = shares[0].shape[1] - LANES
    return call(
        place_body,
        "place",
        [struct((rows, width)), struct((1, rows), F32)],
        [IN_VMEM] * (len(shares) + 1),
        2 * LOC_CAP * rows * width,
        4 * rows * width,
    )(*shares, sel)


def split_cores(core_ref, mine_ref, theirs_ref, cols, block):
    part = mine_ref.shape[0]
    turned = block.T

    @pl.when(core_ref[0] == 0)
    def _():
        mine_ref[:, cols] = turned[:part]
        theirs_ref[:, cols] = turned[part:]

    @pl.when(core_ref[0] == 1)
    def _():
        mine_ref[:, cols] = turned[part:]
        theirs_ref[:, cols] = turned[:part]


def turn_body(chip_ref, core_ref, slices_ref, x_mine, x_theirs, dy_mine, dy_theirs):
    chips, rows, wide = slices_ref.shape
    for key in range(chips):
        cols = slice(key * rows, (key + 1) * rows)
        at = chip_ref[0] ^ key
        split_cores(core_ref, x_mine, x_theirs, cols, slices_ref[at, :, : wide // 2])
        split_cores(core_ref, dy_mine, dy_theirs, cols, slices_ref[at, :, wide // 2 :])


def turn(chip, core, slices):
    chips, rows, wide = slices.shape
    out = (wide // 4, chips * rows)
    return call(
        turn_body,
        "turn",
        [struct(out)] * 4,
        [IN_SMEM] * 2 + [whole(slices.shape)],
        0,
        2 * slices.size,
        grid=(1,),
        out_specs=[whole(out)] * 4,
    )(chip, core, slices)


def stacked(refs):
    return jnp.concatenate([ref[...] for ref in refs], axis=0)


def wide_specs(parts, block):
    return [pl.BlockSpec((part.shape[0], block), lambda j: (0, j)) for part in parts]


def kept(array):
    return pl.BlockSpec(array.shape, lambda j: (0, 0))


def half_specs(parts, block, steps, half):
    at = (lambda j: jnp.minimum(j, steps - 1)) if half == 0 else (lambda j: jnp.maximum(j - steps, 0))
    return [pl.BlockSpec((part.shape[0], block), lambda j: (0, at(j))) for part in parts]


def theirs_body(chips, steps, left_ref, *refs):
    out_ref = refs[-1]
    step = pl.program_id(0)
    for mine, parts in ((step < steps, refs[:chips]), (step >= steps, refs[chips:-1])):

        @pl.when(mine)
        def _():
            out_ref[...] = jnp.dot(
                left_ref[...], stacked(parts), preferred_element_type=F32
            ).astype(BF16)


def theirs_sums(left, parts_a, parts_b):
    part, depth = left.shape
    units = parts_a[0].shape[1]
    block = min(2 * BLOCK, units)
    steps = units // block
    return call(
        functools.partial(theirs_body, len(parts_a), steps),
        "theirs_sums",
        struct((part, 2 * units)),
        [kept(left)] + half_specs(parts_a, block, steps, 0) + half_specs(parts_b, block, steps, 1),
        4 * part * depth * units,
        4 * (depth + part) * units,
        grid=(2 * steps,),
        out_specs=pl.BlockSpec((part, block), lambda j: (0, j)),
        limit=24,
    )(left, *parts_a, *parts_b)


def down_body(inv, chips, steps, left_ref, got_ref, *refs):
    out_ref = refs[-1]
    step = pl.program_id(0)
    for mine, parts in ((step < steps, refs[:chips]), (step >= steps, refs[chips:-1])):

        @pl.when(mine)
        def _():
            total = jnp.dot(left_ref[...], stacked(parts), preferred_element_type=F32)
            out_ref[...] = ((total + got_ref[...].astype(F32)) * inv).T.astype(BF16)


def down_sums(left, got, parts_a, parts_b, inv):
    part, depth = left.shape
    units = parts_a[0].shape[1]
    block = min(2 * BLOCK, units)
    steps = units // block
    return call(
        functools.partial(down_body, inv, len(parts_a), steps),
        "down_sums",
        struct((2 * units, part)),
        [kept(left), pl.BlockSpec((part, block), lambda j: (0, j))]
        + half_specs(parts_a, block, steps, 0)
        + half_specs(parts_b, block, steps, 1),
        4 * part * depth * units,
        4 * (depth + 2 * part) * units,
        grid=(2 * steps,),
        out_specs=pl.BlockSpec((block, part), lambda j: (j, 0)),
        limit=24,
    )(left, got, *parts_a, *parts_b)


def pair_body(inv, chips, steps, left_ref, other_ref, *refs):
    parts, others, (gate_ref, up_ref) = refs[:chips], refs[chips : 2 * chips], refs[-2:]
    total = jnp.dot(left_ref[...], stacked(parts), preferred_element_type=F32)
    total = total + jnp.dot(other_ref[...], stacked(others), preferred_element_type=F32)
    total = (total * inv).astype(BF16)

    @pl.when(pl.program_id(0) < steps)
    def _():
        gate_ref[...] = total

    @pl.when(pl.program_id(0) >= steps)
    def _():
        up_ref[...] = total


def pair_sums(left, other, parts, others, earlier, half, inv):
    part, depth = left.shape
    units = parts[0].shape[1] // 2
    block = min(2 * BLOCK, units)
    steps = units // block
    held = list(earlier)
    count = 2 + 2 * len(parts)
    return call(
        functools.partial(pair_body, inv, len(parts), steps),
        "pair_sums",
        [struct((part, 2 * units))] * 2,
        [kept(left), kept(other)]
        + wide_specs([*parts, *others], block)
        + [pl.BlockSpec(memory_space=pl.ANY)] * len(held),
        8 * part * depth * units,
        8 * (depth + part) * units,
        grid=(2 * steps,),
        out_specs=[
            pl.BlockSpec((part, block), lambda j: (0, half * steps + jnp.minimum(j, steps - 1))),
            pl.BlockSpec((part, block), lambda j: (0, half * steps + jnp.maximum(j - steps, 0))),
        ],
        input_output_aliases={count: 0, count + 1: 1} if held else {},
        limit=24,
    )(left, other, *parts, *others, *held)


def after(value, *earlier):
    return lax.optimization_barrier((value, *earlier))[0]


def shards(tokens, out_grad, route_ids, route_prob, w_gate, w_up, w_down):
    data_ways = lax.axis_size("dp")
    etp_ways = lax.axis_size("etp")
    chips = data_ways // 2
    me = lax.axis_index("dp")
    chip = lax.shift_right_logical(me, 1).reshape(1)
    core = lax.bitwise_and(me, 1).reshape(1)
    inv = 1.0 / data_ways

    x_pack, sel = pack_x(route_ids.T, route_prob.reshape(1, -1), tokens)
    x_blocks = [x_pack] + [shift(x_pack, step) for step in range(1, etp_ways)]
    dy_pack = after(pack_dy(sel, out_grad), *x_blocks[1:])
    dy_blocks = [dy_pack] + [shift(dy_pack, step) for step in range(1, etp_ways)]
    inputs = (x_blocks, [after(x_pack, *dy_blocks[1:]), *x_blocks[1:]])
    scaled, grads, probs, kept_halves = [], [], [], []
    for half in range(2):
        piece, *rest = forward(inputs[half], w_gate, w_up, half)
        scaled.append(chip_gather(piece, chips, half == 1))
        kept_halves.append(rest)
    slices = lax.all_to_all(
        slices_of(x_blocks, dy_blocks, chips),
        "dp",
        split_axis=0,
        concat_axis=0,
        tiled=True,
        axis_index_groups=[[2 * k + at for k in range(chips)] for at in range(2)],
    )
    earlier, later = [], []
    for key in range(1, chips):
        (earlier if key.bit_count() == 1 else later).extend((scaled[0][key], scaled[1][key]))
    parts = []
    for half in range(2):
        hidden, silu, slope = kept_halves[half]
        blocks = [after(dy_blocks[0], *earlier), *dy_blocks[1:]]
        grad, prob = backward(blocks, w_down, hidden, silu, slope, half)
        grads.append(grad)
        probs.append(prob)
        parts.append(chip_gather(grad, chips, half == 1))
        if half == 0:
            first = token_sums(w_gate, w_up, grad, 0, (), etp_ways)
            earlier = [*later, first, parts[0][1], parts[0][chips // 2]]

    probs[0] = after(probs[0], slices)
    shares = token_sums(w_gate, w_up, grads[1], 1, (first, *probs), etp_ways)
    shares = [shares[0]] + [shift(shares[step], -step) for step in range(1, etp_ways)]
    grad_tokens, grad_prob = place(shares, sel)

    x_mine, x_theirs, dy_mine, dy_theirs = turn(chip, core, slices)
    dy_theirs = after(dy_theirs, *shares[1:], *parts[0][1:], *parts[1][1:])
    got = exchange(theirs_sums(dy_theirs, *scaled), 1)
    grad_down = down_sums(dy_mine, got, *scaled, inv)

    far = exchange(after(x_theirs, *shares[1:]), 1)
    held = ()
    for half in range(2):
        others = [
            exchange(after(part, parts[half][-1]) if key.bit_count() < 2 else part, 1)
            for key, part in enumerate(parts[half])
        ]
        if half == 1:
            x_mine = after(x_mine, grad_down)
        held = pair_sums(x_mine, far, parts[half], others, held, half, inv)
    grad_gate, grad_up = held
    return (grad_tokens, grad_prob.reshape(-1), grad_gate, grad_up, grad_down)


def solution(mesh):
    placed = (
        P(("dp", "etp"), None),
        P(("dp", "etp"), None),
        P(("dp", "etp"), None),
        P(("dp", "etp")),
        P(None, "etp"),
        P(None, "etp"),
        P("etp", None),
    )
    return jax.shard_map(
        shards,
        mesh=mesh,
        in_specs=placed,
        out_specs=(
            P(("dp", "etp"), None),
            P(("dp", "etp")),
            P("dp", "etp"),
            P("dp", "etp"),
            P("etp", "dp"),
        ),
        check_vma=False,
    )
```

```python
import functools

import jax
import jax.numpy as jnp
from jax import lax
from jax.experimental import pallas as pl
from jax.experimental.pallas import tpu as pltpu
from jax.sharding import PartitionSpec as P

LOC_CAP = 32
LANES = 128
BLOCK = 256
MIB = 1024 * 1024
BF16 = jnp.bfloat16
F32 = jnp.float32
IN_VMEM = pl.BlockSpec(memory_space=pltpu.VMEM)
IN_HBM = pl.BlockSpec(memory_space=pltpu.HBM)
IN_SMEM = pl.BlockSpec(memory_space=pltpu.SMEM)


def call(body, name, out_shape, in_specs, flops, moved, scratch=(), limit=12, **kwargs):
    if "out_specs" not in kwargs:
        kwargs["out_specs"] = jax.tree.map(lambda _: IN_VMEM, out_shape)
    return pl.pallas_call(
        body,
        out_shape=out_shape,
        in_specs=in_specs,
        scratch_shapes=scratch,
        compiler_params=pltpu.CompilerParams(vmem_limit_bytes=limit * MIB),
        cost_estimate=pl.CostEstimate(
            flops=int(flops), bytes_accessed=int(moved), transcendentals=0
        ),
        name=name,
        **kwargs,
    )


def whole(shape):
    return pl.BlockSpec(shape, lambda *_: (0,) * len(shape))


def struct(shape, kind=BF16):
    return jax.ShapeDtypeStruct(shape, kind)


def nt_dot(left, right):
    return lax.dot_general(left, right, (((1,), (1,)), ((), ())), preferred_element_type=F32)


def shift(block, step):
    ways = lax.axis_size("etp")
    return lax.ppermute(block, "etp", [(i, (i + step) % ways) for i in range(ways)])


def exchange(block, bits):
    ways = lax.axis_size("dp")
    return lax.ppermute(block, "dp", [(i, i ^ bits) for i in range(ways)])


def chip_gather(piece, chips, turned, hold=()):
    bits = [1 << k for k in range(chips.bit_length() - 1)]
    held = {0: piece}
    for bit in bits[::-1] if turned else bits:
        for key in sorted(held):
            held[key ^ bit] = exchange(after(held[key], *hold) if key else held[key], 2 * bit)
    return [held[key] for key in range(chips)]


def pack_x_body(ids_ref, prob_ref, tokens_ref, x_ref, sel_ref):
    rows, width = tokens_ref.shape
    ids = ids_ref[...]
    routed = jnp.logical_or(ids[0:1] == 0, ids[1:2] == 0)
    flags = jnp.broadcast_to(routed.astype(F32), (8, rows)).astype(BF16)
    upto = (
        lax.broadcasted_iota(jnp.int32, (rows, rows), 0)
        <= lax.broadcasted_iota(jnp.int32, (rows, rows), 1)
    ).astype(F32).astype(BF16)
    slot = jnp.dot(flags, upto, preferred_element_type=F32)[0:1].astype(jnp.int32) - 1
    slots = lax.broadcasted_iota(jnp.int32, (LOC_CAP, rows), 0)
    matches = jnp.logical_and(slots == slot, routed)
    sel = matches.astype(F32)
    weight = jnp.sum(sel * prob_ref[...].astype(F32), axis=1, keepdims=True)
    sel = sel.astype(BF16)
    sel_ref[...] = sel
    x_ref[:, :width] = jnp.dot(sel, tokens_ref[...], preferred_element_type=F32).astype(BF16)
    x_ref[:, width:] = jnp.broadcast_to(weight, (LOC_CAP, LANES)).astype(BF16)


def pack_x(ids, prob, tokens):
    rows, width = tokens.shape
    return call(
        pack_x_body,
        "pack_x",
        [struct((LOC_CAP, width + LANES)), struct((LOC_CAP, rows))],
        [IN_VMEM] * 3,
        2 * LOC_CAP * rows * width,
        2 * rows * width,
    )(ids, prob, tokens)


def pack_dy_body(sel_ref, grad_ref, dy_ref):
    dy_ref[...] = jnp.dot(sel_ref[...], grad_ref[...], preferred_element_type=F32).astype(BF16)


def pack_dy(sel, out_grad):
    rows, width = out_grad.shape
    return call(
        pack_dy_body,
        "pack_dy",
        struct((LOC_CAP, width)),
        [IN_VMEM] * 2,
        2 * LOC_CAP * rows * width,
        2 * rows * width,
    )(sel, out_grad)


def slice_body(chips, count, chip_ref, *refs):
    outs = refs[count:]
    wide = outs[0].shape[1]
    for key in range(chips):
        at = pl.multiple_of((chip_ref[0] ^ key) * wide, LANES)
        for z in range(count):
            outs[key][z * LOC_CAP : (z + 1) * LOC_CAP, :] = refs[z][:, pl.ds(at, wide)]


def slices_of(chip, blocks, width, chips):
    count = len(blocks)
    rows = count * LOC_CAP
    return call(
        functools.partial(slice_body, chips, count),
        "slices",
        [struct((rows, width // chips))] * chips,
        [IN_SMEM] + [IN_VMEM] * count,
        0,
        4 * rows * width,
    )(chip, *blocks)


def columns_body(count, *refs):
    out_ref = refs[-1]
    wide = out_ref.shape[2]
    for chip in range(out_ref.shape[0]):
        for z in range(count):
            out_ref[chip, z * LOC_CAP : (z + 1) * LOC_CAP, :] = refs[z][:, chip * wide : (chip + 1) * wide]


def columns_of(blocks, chips):
    count = len(blocks)
    rows = count * LOC_CAP
    width = blocks[0].shape[1]
    return call(
        functools.partial(columns_body, count),
        "columns",
        struct((chips, rows, width // chips)),
        [IN_VMEM] * count,
        0,
        4 * rows * width,
    )(*blocks)


def windowed(groups, sems, ahead):
    made, at = [], 0
    for group in groups:
        made.append(
            [pltpu.make_async_copy(src, dst, sems.at[at + k]) for k, (src, dst) in enumerate(group)]
        )
        at += len(group)
    for copies in made[:ahead]:
        for copy in copies:
            copy.start()
    for step, copies in enumerate(made):
        for copy in copies:
            copy.wait()
        if step + ahead < len(made):
            for copy in made[step + ahead]:
                copy.start()
        yield step


def forward_body(half, count, *refs):
    blocks = refs[:count]
    gate_hbm, up_hbm, scaled_ref, hidden_ref, silu_ref, slope_ref = refs[count : count + 6]
    gate_ref, up_ref, sems = refs[count + 6 :]
    width, units = gate_hbm.shape
    part = units // 2
    block = min(BLOCK, part)
    groups = []
    for at in range(0, part, block):
        src, dst = pl.ds(half * part + at, block), pl.ds(at, block)
        groups.append(
            [(gate_hbm.at[:, src], gate_ref.at[:, dst]), (up_hbm.at[:, src], up_ref.at[:, dst])]
        )
    x = jnp.concatenate([ref[:, :width] for ref in blocks], axis=0)
    weight = jnp.concatenate([ref[:, width : width + 1] for ref in blocks], axis=0).astype(F32)
    for step in windowed(groups, sems, 4):
        cols = slice(step * block, (step + 1) * block)
        gate = jnp.dot(x, gate_ref[:, cols], preferred_element_type=F32)
        up = jnp.dot(x, up_ref[:, cols], preferred_element_type=F32)
        sig = 1.0 / (1.0 + jnp.exp(-gate))
        act = gate * sig
        hidden = (act * up).astype(BF16)
        hidden_ref[:, cols] = hidden
        scaled_ref[:, cols] = (weight * hidden.astype(F32)).astype(BF16)
        silu_ref[:, cols] = weight * act
        slope_ref[:, cols] = weight * up * sig * (1.0 + gate * (1.0 - sig))


def forward(x_blocks, w_gate, w_up, half):
    count = len(x_blocks)
    rows = count * LOC_CAP
    width, units = w_gate.shape
    part = units // 2
    return call(
        functools.partial(forward_body, half, count),
        "forward",
        [struct((rows, part), kind) for kind in (BF16, BF16, F32, F32)],
        [IN_VMEM] * count + [IN_HBM] * 2,
        4 * rows * width * part,
        4 * width * part,
        [pltpu.VMEM((width, part), BF16)] * 2
        + [pltpu.SemaphoreType.DMA((2 * (part // min(BLOCK, part)),))],
        limit=50,
    )(*x_blocks, w_gate, w_up)


def backward_body(half, count, *refs):
    blocks = refs[:count]
    down_hbm, hidden_hbm, silu_hbm, slope_hbm, grad_ref, prob_ref = refs[count : count + 6]
    down_ref, raw_ref, hidden_ref, silu_ref, slope_ref, sems, late_sems = refs[count + 6 :]
    part = hidden_ref.shape[1]
    late = [
        pltpu.make_async_copy(src, dst, late_sems.at[at])
        for at, (src, dst) in enumerate(
            ((hidden_hbm, hidden_ref), (silu_hbm, silu_ref), (slope_hbm, slope_ref))
        )
    ]
    for copy in late:
        copy.start()
    rows, width = pl.ds(half * part, part), down_hbm.shape[1]
    block = 2 * BLOCK
    spans = [pl.ds(at, block) for at in range(0, width, block)]
    groups = [[(down_hbm.at[rows, span], down_ref.at[:, span])] for span in spans]
    for step in windowed(groups, sems, 4):
        cols = slice(step * block, (step + 1) * block)
        dy = jnp.concatenate([ref[:, cols] for ref in blocks], axis=0)
        raw = nt_dot(dy, down_ref[:, cols])
        raw_ref[...] = raw if step == 0 else raw_ref[...] + raw
    for copy in late:
        copy.wait()
    raw = raw_ref[...]
    grad_ref[:, :part] = (raw * slope_ref[...]).astype(BF16)
    grad_ref[:, part:] = (raw * silu_ref[...]).astype(BF16)
    prob_ref[...] = jnp.sum(hidden_ref[...].astype(F32) * raw, axis=1, keepdims=True)


def backward(dy_blocks, w_down, hidden, silu, slope, half):
    count = len(dy_blocks)
    rows, part = hidden.shape
    width = w_down.shape[1]
    return call(
        functools.partial(backward_body, half, count),
        "backward",
        [struct((rows, 2 * part)), struct((rows, 1), F32)],
        [IN_VMEM] * count + [IN_HBM] + [pl.BlockSpec(memory_space=pl.ANY)] * 3,
        2 * rows * width * part,
        2 * width * part + 12 * rows * part,
        [
            pltpu.VMEM((part, width), BF16),
            pltpu.VMEM((rows, part), F32),
            pltpu.VMEM((rows, part), BF16),
            pltpu.VMEM((rows, part), F32),
            pltpu.VMEM((rows, part), F32),
            pltpu.SemaphoreType.DMA((width // (2 * BLOCK),)),
            pltpu.SemaphoreType.DMA((3,)),
        ],
        limit=50,
    )(*dy_blocks, w_down, hidden, silu, slope)


def token_body(half, count, gate_hbm, up_hbm, grad_ref, *refs):
    gate_w, up_w, sems = refs[-3:]
    width, units = gate_hbm.shape
    part = units // 2
    block = min(BLOCK, part)
    groups = []
    for at in range(0, part, block):
        src, dst = pl.ds(half * part + at, block), pl.ds(at, block)
        groups.append(
            [(gate_hbm.at[:, src], gate_w.at[:, dst]), (up_hbm.at[:, src], up_w.at[:, dst])]
        )
    total_ref = refs[0] if half == 0 else refs[-4]
    for step in windowed(groups, sems, 4):
        at = step * block
        cols = slice(at, at + block)
        share = nt_dot(grad_ref[:, cols], gate_w[:, cols])
        share = share + nt_dot(grad_ref[:, part + at : part + at + block], up_w[:, cols])
        total_ref[...] = share if step == 0 else total_ref[...] + share
    if half == 0:
        return
    earlier_ref, prob_a, prob_b = refs[:3]
    outs = refs[3 : 3 + count]
    prob = prob_a[...] + prob_b[...]
    high = prob.astype(BF16).astype(F32)
    mid = (prob - high).astype(BF16).astype(F32)
    low = prob - high - mid
    lane = lax.broadcasted_iota(jnp.int32, (prob.shape[0], LANES), 1)
    terms = jnp.where(
        lane == 0, high, jnp.where(lane == 1, mid, jnp.where(lane == 2, low, 0.0))
    ).astype(BF16)
    for z in range(count):
        rows = slice(z * LOC_CAP, (z + 1) * LOC_CAP)
        outs[z][:, :width] = (total_ref[rows, :] + earlier_ref[rows, :]).astype(BF16)
        outs[z][:, width:] = terms[rows]


def token_sums(w_gate, w_up, grad, half, earlier, count):
    width, units = w_gate.shape
    part = units // 2
    rows = count * LOC_CAP
    weights = [pltpu.VMEM((width, part), BF16)] * 2
    total = [] if half == 0 else [pltpu.VMEM((rows, width), F32)]
    return call(
        functools.partial(token_body, half, count),
        "token_sums",
        struct((rows, width), F32) if half == 0 else [struct((LOC_CAP, width + LANES))] * count,
        [IN_HBM] * 2 + [IN_VMEM] * (1 + len(earlier)),
        4 * rows * width * part,
        4 * width * part,
        total + weights + [pltpu.SemaphoreType.DMA((2 * (part // min(BLOCK, part)),))],
        limit=50,
    )(w_gate, w_up, grad, *earlier)


def place_body(*refs):
    shares, sel_ref, tokens_ref, prob_ref = refs[:-3], refs[-3], refs[-2], refs[-1]
    width = tokens_ref.shape[1]
    total = shares[0][...].astype(F32)
    for share in shares[1:]:
        total = total + share[...].astype(F32)
    rows = total[:, :width].astype(BF16)
    sel = sel_ref[...]
    tokens_ref[...] = lax.dot_general(
        sel, rows, (((0,), (0,)), ((), ())), preferred_element_type=F32
    ).astype(BF16)
    prob = jnp.sum(total[:, width:], axis=1, keepdims=True)
    prob_ref[...] = jnp.sum(jnp.where(sel.astype(F32) > 0.5, prob, 0.0), axis=0, keepdims=True)


def place(shares, sel):
    rows = sel.shape[1]
    width = shares[0].shape[1] - LANES
    return call(
        place_body,
        "place",
        [struct((rows, width)), struct((1, rows), F32)],
        [IN_VMEM] * (len(shares) + 1),
        2 * LOC_CAP * rows * width,
        4 * rows * width,
    )(*shares, sel)


def split_cores(core_ref, mine_ref, theirs_ref, cols, block):
    part = mine_ref.shape[0]
    turned = block.T

    @pl.when(core_ref[0] == 0)
    def _():
        mine_ref[:, cols] = turned[:part]
        theirs_ref[:, cols] = turned[part:]

    @pl.when(core_ref[0] == 1)
    def _():
        mine_ref[:, cols] = turned[part:]
        theirs_ref[:, cols] = turned[:part]


def turn_body(core_ref, *refs):
    slices, (mine_ref, theirs_ref) = refs[:-2], refs[-2:]
    rows = slices[0].shape[0]
    for key, ref in enumerate(slices):
        cols = slice(key * rows, (key + 1) * rows)
        split_cores(core_ref, mine_ref, theirs_ref, cols, ref[...])


def turn(core, slices):
    rows, wide = slices[0].shape
    depth = rows * len(slices)
    out = (wide // 2, depth)
    return call(
        turn_body,
        "turn",
        [struct(out)] * 2,
        [IN_SMEM] + [whole(slices[0].shape)] * len(slices),
        0,
        4 * depth * wide,
        grid=(1,),
        out_specs=[whole(out)] * 2,
    )(core, *slices)


def turn_columns_body(chip_ref, core_ref, columns_ref, mine_ref, theirs_ref):
    chips, rows, _ = columns_ref.shape
    for key in range(chips):
        cols = slice(key * rows, (key + 1) * rows)
        split_cores(core_ref, mine_ref, theirs_ref, cols, columns_ref[chip_ref[0] ^ key])


def turn_columns(chip, core, columns):
    chips, rows, wide = columns.shape
    out = (wide // 2, chips * rows)
    return call(
        turn_columns_body,
        "turn_columns",
        [struct(out)] * 2,
        [IN_SMEM] * 2 + [whole(columns.shape)],
        0,
        2 * columns.size,
        grid=(1,),
        out_specs=[whole(out)] * 2,
    )(chip, core, columns)


def stacked(refs):
    return jnp.concatenate([ref[...] for ref in refs], axis=0)


def wide_specs(parts, block):
    return [pl.BlockSpec((part.shape[0], block), lambda j: (0, j)) for part in parts]


def kept(array):
    return pl.BlockSpec(array.shape, lambda j: (0, 0))


def half_specs(parts, block, steps, half):
    at = (lambda j: jnp.minimum(j, steps - 1)) if half == 0 else (lambda j: jnp.maximum(j - steps, 0))
    return [pl.BlockSpec((part.shape[0], block), lambda j: (0, at(j))) for part in parts]


def theirs_body(chips, steps, left_ref, *refs):
    out_ref = refs[-1]
    step = pl.program_id(0)
    for mine, parts in ((step < steps, refs[:chips]), (step >= steps, refs[chips:-1])):

        @pl.when(mine)
        def _():
            out_ref[...] = jnp.dot(
                left_ref[...], stacked(parts), preferred_element_type=F32
            ).astype(BF16)


def theirs_sums(left, parts_a, parts_b):
    part, depth = left.shape
    units = parts_a[0].shape[1]
    block = min(2 * BLOCK, units)
    steps = units // block
    return call(
        functools.partial(theirs_body, len(parts_a), steps),
        "theirs_sums",
        struct((part, 2 * units)),
        [kept(left)] + half_specs(parts_a, block, steps, 0) + half_specs(parts_b, block, steps, 1),
        4 * part * depth * units,
        4 * (depth + part) * units,
        grid=(2 * steps,),
        out_specs=pl.BlockSpec((part, block), lambda j: (0, j)),
        limit=24,
    )(left, *parts_a, *parts_b)


def down_body(inv, chips, steps, left_ref, got_ref, *refs):
    out_ref = refs[-1]
    step = pl.program_id(0)
    for mine, parts in ((step < steps, refs[:chips]), (step >= steps, refs[chips:-1])):

        @pl.when(mine)
        def _():
            total = jnp.dot(left_ref[...], stacked(parts), preferred_element_type=F32)
            out_ref[...] = ((total + got_ref[...].astype(F32)) * inv).T.astype(BF16)


def down_sums(left, got, parts_a, parts_b, inv):
    part, depth = left.shape
    units = parts_a[0].shape[1]
    block = min(2 * BLOCK, units)
    steps = units // block
    return call(
        functools.partial(down_body, inv, len(parts_a), steps),
        "down_sums",
        struct((2 * units, part)),
        [kept(left), pl.BlockSpec((part, block), lambda j: (0, j))]
        + half_specs(parts_a, block, steps, 0)
        + half_specs(parts_b, block, steps, 1),
        4 * part * depth * units,
        4 * (depth + 2 * part) * units,
        grid=(2 * steps,),
        out_specs=pl.BlockSpec((block, part), lambda j: (j, 0)),
        limit=24,
    )(left, got, *parts_a, *parts_b)


def pair_body(inv, chips, steps, left_ref, other_ref, *refs):
    parts, others, (gate_ref, up_ref) = refs[:chips], refs[chips : 2 * chips], refs[-2:]
    total = jnp.dot(left_ref[...], stacked(parts), preferred_element_type=F32)
    total = total + jnp.dot(other_ref[...], stacked(others), preferred_element_type=F32)
    total = (total * inv).astype(BF16)

    @pl.when(pl.program_id(0) < steps)
    def _():
        gate_ref[...] = total

    @pl.when(pl.program_id(0) >= steps)
    def _():
        up_ref[...] = total


def pair_sums(left, other, parts, others, earlier, half, inv):
    part, depth = left.shape
    units = parts[0].shape[1] // 2
    block = min(2 * BLOCK, units)
    steps = units // block
    held = list(earlier)
    count = 2 + 2 * len(parts)
    return call(
        functools.partial(pair_body, inv, len(parts), steps),
        "pair_sums",
        [struct((part, 2 * units))] * 2,
        [kept(left), kept(other)]
        + wide_specs([*parts, *others], block)
        + [pl.BlockSpec(memory_space=pl.ANY)] * len(held),
        8 * part * depth * units,
        8 * (depth + part) * units,
        grid=(2 * steps,),
        out_specs=[
            pl.BlockSpec((part, block), lambda j: (0, half * steps + jnp.minimum(j, steps - 1))),
            pl.BlockSpec((part, block), lambda j: (0, half * steps + jnp.maximum(j - steps, 0))),
        ],
        input_output_aliases={count: 0, count + 1: 1} if held else {},
        limit=24,
    )(left, other, *parts, *others, *held)


def after(value, *earlier):
    return lax.optimization_barrier((value, *earlier))[0]


def shards(tokens, out_grad, route_ids, route_prob, w_gate, w_up, w_down):
    data_ways = lax.axis_size("dp")
    etp_ways = lax.axis_size("etp")
    chips = data_ways // 2
    me = lax.axis_index("dp")
    chip = lax.shift_right_logical(me, 1).reshape(1)
    core = lax.bitwise_and(me, 1).reshape(1)
    inv = 1.0 / data_ways

    x_pack, sel = pack_x(route_ids.T, route_prob.reshape(1, -1), tokens)
    x_blocks = [x_pack] + [shift(x_pack, step) for step in range(1, etp_ways)]
    dy_pack = after(pack_dy(sel, out_grad), *x_blocks[1:])
    dy_blocks = [dy_pack] + [shift(dy_pack, step) for step in range(1, etp_ways)]
    width = tokens.shape[1]
    x_slices = slices_of(chip, x_blocks, width, chips)
    x_slices = [x_slices[0]] + [exchange(x_slices[key], 2 * key) for key in range(1, chips)]
    near = [x_slices[1 << k] for k in range(chips.bit_length() - 1)]
    inputs = (x_blocks, [after(x_pack, *near, *dy_blocks[1:]), *x_blocks[1:]])
    scaled, grads, probs, kept_halves = [], [], [], []
    for half in range(2):
        piece, *rest = forward(inputs[half], w_gate, w_up, half)
        scaled.append(chip_gather(piece, chips, half == 1))
        kept_halves.append(rest)
    earlier = [*x_slices[1:], *scaled[0][1:]]
    earlier += [scaled[1][key] for key in range(1, chips) if key.bit_count() == 1]
    later = [scaled[1][key] for key in range(1, chips) if key.bit_count() > 1]
    parts = []
    for half in range(2):
        hidden, silu, slope = kept_halves[half]
        blocks = [after(dy_blocks[0], *earlier), *dy_blocks[1:]]
        grad, prob = backward(blocks, w_down, hidden, silu, slope, half)
        grads.append(grad)
        probs.append(prob)
        if half == 0:
            first = token_sums(w_gate, w_up, grad, 0, (), etp_ways)
            parts.append(chip_gather(grad, chips, False, (first,)))
            earlier = [*later, first, parts[0][1], parts[0][chips // 2]]
    dy_columns = lax.all_to_all(
        columns_of([after(dy_blocks[0], probs[0]), *dy_blocks[1:]], chips),
        "dp",
        split_axis=0,
        concat_axis=0,
        tiled=True,
        axis_index_groups=[[2 * k + at for k in range(chips)] for at in range(2)],
    )

    shares = token_sums(w_gate, w_up, grads[1], 1, (first, *probs), etp_ways)
    parts.append(chip_gather(grads[1], chips, True, (shares[0],)))
    shares = [shares[0]] + [shift(shares[step], -step) for step in range(1, etp_ways)]
    grad_tokens, grad_prob = place(shares, sel)

    x_mine, x_theirs = turn(core, x_slices)
    dy_mine, dy_theirs = turn_columns(chip, core, dy_columns)
    dy_theirs = after(dy_theirs, *shares[1:], *parts[0][1:], *parts[1][1:])
    got = exchange(theirs_sums(dy_theirs, *scaled), 1)
    grad_down = down_sums(dy_mine, got, *scaled, inv)

    far = exchange(after(x_theirs, *shares[1:]), 1)
    held = ()
    for half in range(2):
        others = [
            exchange(after(part, parts[half][-1]) if key.bit_count() < 2 else part, 1)
            for key, part in enumerate(parts[half])
        ]
        if half == 1:
            x_mine = after(x_mine, grad_down)
        held = pair_sums(x_mine, far, parts[half], others, held, half, inv)
    grad_gate, grad_up = held
    return (grad_tokens, grad_prob.reshape(-1), grad_gate, grad_up, grad_down)


def solution(mesh):
    placed = (
        P(("dp", "etp"), None),
        P(("dp", "etp"), None),
        P(("dp", "etp"), None),
        P(("dp", "etp")),
        P(None, "etp"),
        P(None, "etp"),
        P("etp", None),
    )
    return jax.shard_map(
        shards,
        mesh=mesh,
        in_specs=placed,
        out_specs=(
            P(("dp", "etp"), None),
            P(("dp", "etp")),
            P("dp", "etp"),
            P("dp", "etp"),
            P("etp", "dp"),
        ),
        check_vma=False,
    )
```
